256 devices in a mesh: dom: 64 (over y, z, core), kv: 4 (over x).
Axes of the slice: x: 4, y: 4, z: 8, core: 2. Of those that a mesh axis runs over, the one named last changes fastest.
Arguments:
- node_feats: bfloat16 [32768, 128], P(('dom', 'kv')), may hold values from -11 to 11
- positions: float32 [3, 32768], P(None, ('dom', 'kv')), may hold values from 0 to 2304, as said below
- species: int32 [32768], P(('dom', 'kv')), may hold values from 0 to 1
- halo_rows: int32 [256, 64], P(('dom', 'kv')), may hold values from 0 to 127, as said below
- neighbours: int32 [32768, 32], P(('dom', 'kv')), may hold values from 0 to 191, as said below
- nbr_count: int32 [32768], P(('dom', 'kv')), may hold values from 16 to 32, as said below
- recip_vectors: int32 [3, 16384], replicated, may hold values from -13 to 13, as said below
- w_msg: bfloat16 [128, 128], replicated, may hold values from -0.5 to 0.5
- w_rad1: bfloat16 [8, 128], replicated, may hold values from -2 to 2
- w_rad2: bfloat16 [128, 256], replicated, may hold values from -0.5 to 0.5
- w_upd: bfloat16 [384, 128], replicated, may hold values from -0.3125 to 0.3125
- w_out: bfloat16 [128], replicated, may hold values from -0.5 to 0.5
- chi_table: float32 [2], replicated, may hold values from -1 to 1
- hard_table: float32 [2], replicated, may hold values from 0.5 to 2
Outputs:
- electroneg: float32 [32768], P(('dom', 'kv'))
- charges: float32 [32768], P(('dom', 'kv'))
The draws below stay inside these ranges and needn't reach their ends.
Inputs may be any that keep to these rules, and one draw needn't show every extreme that they name: `halo_rows`: in each slab's row, 64 distinct local atom indices; the first 32 lie near the slab's lower face, the rest near its upper face. `neighbours`: an atom never lists its own local index. `nbr_count`: the first atom of every slab has all 32 slots live. `recip_vectors`: distinct nonzero triples. `positions`: atoms of slab s have first coordinate in [9 s, 9 (s + 1)), the other two in [0, 20).
All inputs are finite; a program needn't handle non-finite values.
Results may differ from the reference program's by a relative error of at most 0.003.
Values may be sent and summed in bfloat16 or wider, within the bound.
A program may use at most 128 MiB of HBM per device.

```python
import math
import jax
import jax.numpy as jnp
from jax import lax

ATOM_DEV = 128
C = 128
NBR = 32
RB = 8
SPECIES = 2
KVEC = 16384
ITERS = 4
HALO = 32
SLABS = 256
ATOMS = 32768
N_DOM = 64
N_KV = 4


def layout_helper(key):
    slab_keys = jax.random.split(jax.random.fold_in(key, 11), SLABS)
    send_rows = jax.vmap(lambda slab_key: jax.random.permutation(slab_key, ATOM_DEV)[:2 * HALO])(slab_keys).astype(jnp.int32)
    slab_ids = jnp.arange(SLABS)[:, None]
    face_marks = jnp.zeros((SLABS, ATOM_DEV), jnp.int32)
    face_marks = face_marks.at[slab_ids, send_rows[:, :HALO]].set(1)
    face_marks = face_marks.at[slab_ids, send_rows[:, HALO:]].set(2)
    uniform_draw = jax.random.uniform(jax.random.fold_in(key, 12), (3, SLABS, ATOM_DEV), jnp.float32)
    fraction = jnp.where(face_marks == 1, 0.3 * uniform_draw[0], jnp.where(face_marks == 2, 0.7 + 0.3 * uniform_draw[0], uniform_draw[0]))
    coord_x = (jnp.arange(SLABS, dtype=jnp.float32)[:, None] + fraction) * 9.0
    coord_y = uniform_draw[1] * 20.0
    coord_z = uniform_draw[2] * 20.0
    coords = jnp.stack([coord_x, coord_y, coord_z]).reshape(3, ATOMS)
    return (send_rows, coords)


def draw_halo_rows(key, part):
    return layout_helper(key)[0]


def draw_positions(key, part):
    return layout_helper(key)[1].astype(jnp.float32)


def draw_neighbours(key, part):
    raw_index = jax.random.randint(jax.random.fold_in(key, 21), (ATOMS, NBR), 0, ATOM_DEV + 2 * HALO - 1)
    own_index = (jnp.arange(ATOMS) % ATOM_DEV)[:, None]
    return jnp.where(raw_index >= own_index, raw_index + 1, raw_index).astype(jnp.int32)


def draw_nbr_count(key, part):
    raw_count = jax.random.randint(jax.random.fold_in(key, 31), (ATOMS,), NBR // 2, NBR + 1)
    return jnp.where(jnp.arange(ATOMS) % ATOM_DEV == 0, NBR, raw_count).astype(jnp.int32)


def draw_recip_vectors(key, part):
    cube_cells = 27 * 27 * 27 - 1
    cube_centre = cube_cells // 2
    shuffled = jax.random.permutation(jax.random.fold_in(key, 41), cube_cells)[:KVEC]
    cell_index = shuffled + (shuffled >= cube_centre).astype(shuffled.dtype)
    triples = jnp.stack([cell_index // 729 - 13, cell_index // 27 % 27 - 13, cell_index % 27 - 13])
    return triples.astype(jnp.int32)


def draw_node_feats(key, part):
    slab_index = (jnp.arange(ATOMS) // ATOM_DEV).astype(jnp.float32)
    values = jnp.clip(jax.random.normal(jax.random.fold_in(key, 53), (ATOMS, C), jnp.float32), -4.0, 4.0)
    ramp_scale = 0.5 + slab_index / (SLABS - 1)
    return (values * ramp_scale[:, None]).astype(jnp.bfloat16)


def touch_ends(drawn, own_key, smallest, largest):
    place = [jax.random.randint(jax.random.fold_in(own_key, axis), (), 0, length) for axis, length in enumerate(drawn.shape)]
    widest = drawn.shape.index(max(drawn.shape))
    beside = place[:widest] + [(place[widest] + 1) % drawn.shape[widest]] + place[widest + 1:]
    return drawn.at[tuple(place)].set(smallest).at[tuple(beside)].set(largest)


def bell_draw(key, shape, deviation, reach, kind=jnp.bfloat16):
    entries = deviation * jax.random.normal(key, shape, jnp.float32)
    return jnp.clip(entries, min=-reach, max=reach).astype(kind)


def setup_inputs(seed: int = 0) -> dict:
    seeds = jax.random.split(jax.random.key(seed), 15)
    return {
        "node_feats": draw_node_feats(jax.random.fold_in(seeds[14], 71), 0),
        "positions": draw_positions(jax.random.fold_in(seeds[14], 71), 0),
        "species": touch_ends(jax.random.randint(seeds[2], (ATOMS,), 0, SPECIES), jax.random.fold_in(seeds[2], 1), 0, SPECIES - 1).astype(jnp.int32),
        "halo_rows": draw_halo_rows(jax.random.fold_in(seeds[14], 71), 0),
        "neighbours": draw_neighbours(jax.random.fold_in(seeds[14], 71), 0),
        "nbr_count": draw_nbr_count(jax.random.fold_in(seeds[14], 71), 0),
        "recip_vectors": draw_recip_vectors(jax.random.fold_in(seeds[14], 71), 0),
        "w_msg": bell_draw(seeds[7], (C, C), C ** -0.5, 0.5),
        "w_rad1": bell_draw(seeds[8], (RB, C), RB ** -0.5, 2.0),
        "w_rad2": bell_draw(seeds[9], (C, 2 * C), C ** -0.5, 0.5),
        "w_upd": bell_draw(seeds[10], (3 * C, C), (3 * C) ** -0.5, 0.3125),
        "w_out": bell_draw(seeds[11], (C,), C ** -0.5, 0.5),
        "chi_table": jnp.clip(jax.random.uniform(seeds[12], (SPECIES,), jnp.float32, -1.0, 1.0), -1.0, 1.0),
        "hard_table": jnp.clip(jnp.exp(jax.random.uniform(seeds[13], (SPECIES,), jnp.float32, math.log(0.5), math.log(2.0))), 0.5, 2.0),
    }


slab_width = 9.0
side_length = 20.0
two_pi = 2.0 * math.pi
highest = lax.Precision.HIGHEST

def wrapped(offset, length):
    return jnp.where(offset > 0.5 * length, offset - length, jnp.where(offset < -0.5 * length, offset + length, offset))

def recip_setup(coords, triples, box_x, atoms_total):
    comp_x = triples[0].astype(jnp.float32)
    comp_y = triples[1].astype(jnp.float32)
    comp_z = triples[2].astype(jnp.float32)
    phase_arg = two_pi * (coords[0][:, None] * (comp_x / box_x)[None, :] + coords[1][:, None] * (comp_y / side_length)[None, :] + coords[2][:, None] * (comp_z / side_length)[None, :])
    phase_table = jnp.concatenate([jnp.cos(phase_arg), jnp.sin(phase_arg)], axis=1)
    m_square = comp_x * comp_x + comp_y * comp_y + comp_z * comp_z
    weight = 16.0 / atoms_total * jnp.exp(-m_square / 400.0) / (1.0 + m_square / 16.0)
    return (phase_table, weight)

def message_layer(ext_proj, ext_pos, own_pos, own_feats, nbr_index, counts, kinds, w_rad1, w_rad2, w_upd, w_out, chi_table, box_x):
    atoms_dev, slot_count = nbr_index.shape
    channels = own_feats.shape[1]
    flat_index = nbr_index.reshape(-1)
    nbr_proj = jnp.take(ext_proj, flat_index, axis=0).reshape(atoms_dev, slot_count, channels)
    nbr_pos = jnp.take(ext_pos, flat_index, axis=1).reshape(3, atoms_dev, slot_count)
    displace = jnp.stack([wrapped(nbr_pos[0] - own_pos[0][:, None], box_x), wrapped(nbr_pos[1] - own_pos[1][:, None], side_length), wrapped(nbr_pos[2] - own_pos[2][:, None], side_length)])
    distance = jnp.sqrt(lax.optimization_barrier(jnp.sum(displace * displace, axis=0)) + 0.25)
    unit_vec = displace / distance
    basis_count = w_rad1.shape[0]
    centres = 1.0 + 1.25 * jnp.arange(basis_count, dtype=jnp.float32)
    radial_basis = jnp.exp(-jnp.square((distance[:, :, None] - centres) / 1.25)).astype(jnp.bfloat16)
    hidden = jax.nn.silu(jnp.dot(radial_basis.reshape(-1, basis_count), w_rad1, preferred_element_type=jnp.float32)).astype(jnp.bfloat16)
    radial = jnp.dot(hidden, w_rad2, preferred_element_type=jnp.float32).reshape(atoms_dev, slot_count, 2 * channels)
    live_mask = (jnp.arange(slot_count)[None, :] < counts[:, None]).astype(jnp.float32)
    radial = radial * live_mask[:, :, None]
    msg_scale = 1.0 / math.sqrt(slot_count)
    scalar_msg = lax.optimization_barrier(jnp.sum(radial[:, :, :channels] * nbr_proj, axis=1)) * msg_scale
    carried = radial[:, :, channels:] * nbr_proj
    vector_msg = lax.optimization_barrier(jnp.sum(unit_vec[:, :, :, None] * carried[None], axis=2)) * msg_scale
    vec_square = lax.optimization_barrier(jnp.sum(vector_msg * vector_msg, axis=0))
    joined = jnp.concatenate([scalar_msg, vec_square, own_feats.astype(jnp.float32)], axis=1).astype(jnp.bfloat16)
    update = jax.nn.silu(jnp.dot(joined, w_upd, preferred_element_type=jnp.float32)).astype(jnp.bfloat16)
    one_hot = (kinds[:, None] == jnp.arange(chi_table.shape[0])[None, :]).astype(jnp.float32)
    return jnp.dot(update, w_out, preferred_element_type=jnp.float32) + lax.optimization_barrier(jnp.sum(one_hot * chi_table[None, :], axis=1))

def reference(node_feats, positions, species, halo_rows, neighbours, nbr_count, recip_vectors, w_msg, w_rad1, w_rad2, w_upd, w_out, chi_table, hard_table):
    slab_count = N_DOM * N_KV
    box_x = slab_count * slab_width
    slab_feats = node_feats.reshape(slab_count, ATOM_DEV, C)
    slab_pos = positions.reshape(3, slab_count, ATOM_DEV)
    sent_feats = jnp.take_along_axis(slab_feats, halo_rows[:, :, None], axis=1)
    sent_pos = jnp.take_along_axis(slab_pos, jnp.broadcast_to(halo_rows[None, :, :], (3, slab_count, 2 * HALO)), axis=2)
    ext_f = jnp.concatenate([slab_feats, jnp.roll(sent_feats[:, HALO:], 1, axis=0), jnp.roll(sent_feats[:, :HALO], -1, axis=0)], axis=1)
    ext_p = jnp.concatenate([slab_pos, jnp.roll(sent_pos[:, :, HALO:], 1, axis=1), jnp.roll(sent_pos[:, :, :HALO], -1, axis=1)], axis=2)
    ext_p = jnp.transpose(ext_p, (1, 0, 2))
    own_all = jnp.transpose(slab_pos, (1, 0, 2))

    def one_slab(slab_args):
        feats_ext, pos_ext, own_pos, own_feats, nbr_index, counts, kinds = slab_args
        ext_proj = jnp.dot(feats_ext, w_msg, preferred_element_type=jnp.float32).astype(jnp.bfloat16)
        return message_layer(ext_proj, pos_ext, own_pos, own_feats, nbr_index, counts, kinds, w_rad1, w_rad2, w_upd, w_out, chi_table, box_x)
    electroneg = lax.map(one_slab, (ext_f, ext_p, own_all, slab_feats, neighbours.reshape(slab_count, ATOM_DEV, NBR), nbr_count.reshape(slab_count, ATOM_DEV), species.reshape(slab_count, ATOM_DEV))).reshape(ATOMS)
    one_hot = (species[:, None] == jnp.arange(SPECIES)[None, :]).astype(jnp.float32)
    hardness = lax.optimization_barrier(jnp.sum(one_hot * hard_table[None, :], axis=1))
    block_size = math.gcd(KVEC, 512)
    k_blocks = jnp.transpose(recip_vectors.reshape(3, KVEC // block_size, block_size), (1, 0, 2))

    def apply_operator(direction):

        def add_block(running, trip_block):
            phase_table, weight = recip_setup(positions, trip_block, box_x, ATOMS)
            weight_pair = jnp.concatenate([weight, weight])
            partial_value = jnp.dot(direction, phase_table, precision=highest, preferred_element_type=jnp.float32)
            spread = lax.dot_general(partial_value * weight_pair, phase_table, (((1,), (1,)), ((), ())), precision=highest, preferred_element_type=jnp.float32)
            return (running + spread, None)
        potential, _ = lax.scan(add_block, jnp.zeros((2, ATOMS), jnp.float32), k_blocks)
        return hardness * direction + potential
    right_side = jnp.stack([-electroneg, jnp.ones((ATOMS,), jnp.float32)])
    solution = jnp.zeros((2, ATOMS), jnp.float32)
    residual = right_side
    direction = right_side
    norm_now = lax.optimization_barrier(jnp.sum(residual * residual, axis=1))
    for iteration in range(ITERS):
        applied = apply_operator(direction)
        step_size = norm_now / lax.optimization_barrier(jnp.sum(direction * applied, axis=1))
        solution = solution + step_size[:, None] * direction
        residual = residual - step_size[:, None] * applied
        norm_next = lax.optimization_barrier(jnp.sum(residual * residual, axis=1))
        direction = residual + (norm_next / norm_now)[:, None] * direction
        norm_now = norm_next
    totals = lax.optimization_barrier(jnp.sum(solution, axis=1))
    charges = solution[0] - totals[0] / totals[1] * solution[1]
    return (electroneg, charges)
```

```python
import functools
import math

import jax
import jax.numpy as jnp
from jax import lax
from jax.experimental import pallas as pl
from jax.experimental.pallas import tpu as pltpu
from jax.sharding import PartitionSpec as P

MESH = pl.DeviceIdType.MESH
F32, BF16, I32 = jnp.float32, jnp.bfloat16, jnp.int32
ITERS = 4
SLAB_W = 9.0
SIDE = 20.0
A = 128
NBR = 32
HALF = 384
ROWS = 6 * 64
TROWS = 160
TURN = 2.0 * math.pi
SIN_C = [(-1.0) ** k * TURN ** (2 * k + 1) / math.factorial(2 * k + 1) for k in range(10)]
COS_C = [(-1.0) ** k * TURN ** (2 * k) / math.factorial(2 * k) for k in range(10)]


def dot(a, b):
    return jnp.dot(a, b, preferred_element_type=F32)


def dot_nt(a, b):
    return lax.dot_general(a, b, (((1,), (1,)), ((), ())), preferred_element_type=F32)


def sincos(turns):
    t = turns - jnp.round(turns)
    q = t * t
    s = jnp.full_like(q, SIN_C[-1])
    c = jnp.full_like(q, COS_C[-1])
    for k in range(len(SIN_C) - 2, -1, -1):
        s = s * q + SIN_C[k]
        c = c * q + COS_C[k]
    return s * t, c


def silu(v):
    h = 0.5 * v
    return h + h * jnp.tanh(h)


def transposed(v):
    return v.astype(F32).T


def iota(shape, dim):
    return lax.broadcasted_iota(I32, shape, dim)


class Grid:
    def __init__(self, sizes):
        self.sizes = sizes
        ny, nz, nc, nx = sizes
        dom, x = lax.axis_index("dom"), lax.axis_index("kv")
        self.y, self.z, self.c, self.x = dom // (nz * nc), (dom // nc) % nz, dom % nc, x
        self.dom = dom
        self.reduce_count = nx * ny
        self.gather_count = nz * nc
        self.reduce_id = self.y * nx + self.x
        self.gather_id = self.z * nc + self.c

    def reduce_peer(self, index):
        ny, nz, nc, nx = self.sizes
        return {"dom": ((index // nx) * nz + self.z) * nc + self.c, "kv": index % nx}

    def gather_peer(self, index):
        ny, nz, nc, nx = self.sizes
        return {"dom": self.y * (nz * nc) + index, "kv": self.x}

    def slab_peer(self, step):
        ny, nz, nc, nx = self.sizes
        count = ny * nz * nc * nx
        slab = (self.dom * nx + self.x + step + count) % count
        return {"dom": slab // nx, "kv": slab % nx}


def kernel(
    sizes,
    feats_ref,
    pos_ref,
    species_ref,
    halo_ref,
    nbr_ref,
    count_ref,
    recip_ref,
    w_msg_ref,
    w_rad1_ref,
    w_rad2_ref,
    w_upd_ref,
    w_out_ref,
    chi_ref,
    hard_ref,
    en_ref,
    charge_ref,
    own_tab,
    packet,
    got,
    pos_all,
    en_all,
    nbr_tab,
    slots,
    acc,
    w_rad1_t,
    w_rad2_t,
    w_upd_t,
    table,
    xfac,
    hard_all,
    ff,
    res,
    direc,
    sol,
    pay,
    recv,
    full,
    present,
    w_sum,
    w_dif,
    s_dir,
    halo_sem,
    pos_sem,
    en_sem,
    rs_sem,
    ag_sem,
):
    grid = Grid(sizes)
    gcount, rcount = grid.gather_count, grid.reduce_count
    gid, rid = grid.gather_id, grid.reduce_id
    atoms = gcount * A
    atoms_total = atoms * rcount
    box_x = (atoms_total // A) * SLAB_W
    chunk = ROWS // rcount
    kvec = recip_ref.shape[1]

    barrier = pltpu.get_barrier_semaphore()

    def greet(device):
        pl.semaphore_signal(barrier, inc=1, device_id=device, device_id_type=MESH)

    greet(grid.slab_peer(-1))
    greet(grid.slab_peer(1))
    for d in range(1, gcount):
        greet(grid.gather_peer((gid + d) % gcount))
    for d in range(1, rcount):
        greet(grid.reduce_peer((rid + d) % rcount))

    def remote(src, dst, send, recv_, device):
        return pltpu.make_async_remote_copy(
            src_ref=src, dst_ref=dst, send_sem=send, recv_sem=recv_, device_id=device, device_id_type=MESH
        )

    def own_rows(ref, rnd, index):
        return ref.at[rnd, pl.ds(pl.multiple_of(index * chunk, 8), chunk)]

    species = species_ref[...]
    hardness = jnp.where(species == 0, hard_ref[0], hard_ref[1])
    pos = jnp.concatenate([pos_ref[...], jnp.zeros((5, A), F32)], axis=0)
    pos_all[gid] = jnp.concatenate([pos_ref[...], hardness, jnp.zeros((4, A), F32)], axis=0)
    feats_t = transposed(feats_ref[...])
    proj_t = dot(transposed(w_msg_ref[...]).astype(BF16), feats_t.astype(BF16))
    hi = pos.astype(BF16).astype(F32)
    mid = (pos - hi).astype(BF16).astype(F32)
    low = pos - hi - mid
    own_tab[...] = jnp.concatenate([proj_t, hi, mid, low, jnp.zeros((8, A), F32)], axis=0).astype(BF16)
    halo = jnp.concatenate([halo_ref[...], halo_ref[...]], axis=1)
    pick = jnp.where(iota((A, A), 0) == halo, 1.0, 0.0).astype(BF16)
    packet[...] = dot(own_tab[...], pick).astype(BF16)

    k_step = 2048 if kvec % 2048 == 0 else kvec
    present[...] = jnp.zeros((32, HALF), F32)

    def count_triples(step, carry):
        m = recip_ref[:, pl.ds(pl.multiple_of(step * k_step, 128), k_step)]
        mx, my, mz = m[0:1], m[1:2], m[2:3]
        flip = jnp.where((my < 0) | ((my == 0) & (mz < 0)), -1, 1)
        mx, my, mz = mx * flip, my * flip, mz * flip + 13
        row = jnp.where(mx >= 0, mx, 16 - mx)
        column = jnp.where(mz < 24, my * 24 + mz, 336 + (mz - 24) * 16 + my)
        hot_row = jnp.where(iota((32, k_step), 0) == row, 1.0, 0.0).astype(BF16)
        hot_col = jnp.where(iota((HALF, k_step), 0) == column, 1.0, 0.0).astype(BF16)
        present[...] += dot_nt(hot_row, hot_col)
        return carry

    k_steps = kvec // k_step
    lax.fori_loop(0, k_steps // 2, count_triples, 0)

    pl.semaphore_wait(barrier, 2 + gcount - 1 + rcount - 1)

    to_left = remote(packet, got.at[1], halo_sem.at[0], halo_sem.at[3], grid.slab_peer(-1))
    to_right = remote(packet, got.at[0], halo_sem.at[1], halo_sem.at[2], grid.slab_peer(1))
    to_left.start()
    to_right.start()
    for d in range(1, gcount):
        peer = grid.gather_peer((gid + d) % gcount)
        remote(pos_all.at[gid], pos_all.at[gid], pos_sem.at[0], pos_sem.at[1], peer).start()

    lax.fori_loop(k_steps // 2, k_steps, count_triples, 0)
    column = iota((1, HALF), 1)
    late = column - 336
    grid_y = jnp.where(late < 0, (column * 2731) >> 16, late & 15)
    grid_z = jnp.where(late < 0, column - grid_y * 24 - 13, 11 + (late >> 4))
    grid_x = iota((16, 1), 0)
    m_square = (grid_y * grid_y + grid_z * grid_z + grid_x * grid_x).astype(F32)
    weight = 16.0 / atoms_total * jnp.exp(-m_square / 400.0) / (1.0 + m_square / 16.0)
    plus, minus = present[0:16] * weight, present[16:32] * weight
    for i in range(3):
        lanes = slice(i * 128, (i + 1) * 128)
        w_sum[i] = (plus + minus)[:, lanes]
        w_dif[i] = (plus - minus)[:, lanes]

    w_rad1_t[...] = jnp.concatenate(
        [transposed(jnp.concatenate([w_rad1_ref[...].astype(F32), jnp.zeros((120, A), F32)], axis=0))], axis=1
    ).astype(BF16)
    for i in range(2):
        w_rad2_t[pl.ds(i * A, A), :] = transposed(w_rad2_ref[:, i * A : (i + 1) * A]).astype(BF16)
    for i in range(3):
        w_upd_t[:, pl.ds(i * A, A)] = transposed(w_upd_ref[i * A : (i + 1) * A, :]).astype(BF16)
    index = jnp.concatenate([nbr_ref[...].astype(F32), jnp.zeros((A, A - NBR), F32)], axis=1).T[0:NBR].astype(I32)
    place = jnp.where(index < A, index, jnp.where(index < A + 32, index + 32, index - 32))
    slots[...] = jnp.where(iota((NBR, A), 0) < count_ref[...], place, -1)
    nbr_tab[:, 0:A] = own_tab[...]

    to_left.wait_send()
    to_right.wait_send()
    to_left.wait_recv()
    to_right.wait_recv()
    from_right, from_left = got[1].astype(F32), got[0].astype(F32)
    nbr_tab[:, A : 2 * A] = jnp.where(iota((TROWS, A), 1) < 32, from_right, from_left).astype(BF16)

    group = 4
    wide = group * A
    acc[...] = jnp.zeros(acc.shape, F32)
    own_pos = jnp.concatenate([pos] * group, axis=1)
    axis_row = iota((8, 1), 0)
    length = jnp.where(axis_row == 0, box_x, SIDE)
    live_row = axis_row < 3

    def messages(step, carry):
        here = jnp.concatenate([slots[pl.ds(step * group + s, 1), :] for s in range(group)], axis=1)
        hot = jnp.where(iota((2 * A, wide), 0) == here, 1.0, 0.0).astype(BF16)
        found = dot(nbr_tab[...], hot)
        proj = found[0:A]
        offset = found[A : A + 8] + found[A + 8 : A + 16] + found[A + 16 : A + 24] - own_pos
        offset = jnp.where(
            offset > 0.5 * length, offset - length, jnp.where(offset < -0.5 * length, offset + length, offset)
        )
        offset = jnp.where(live_row, offset, 0.0)
        square = jnp.sum(offset * offset, axis=0, keepdims=True) + 0.25
        inverse = lax.rsqrt(square)
        unit = offset * inverse
        distance = square * inverse
        centre = 1.0 + 1.25 * iota((8, 1), 0).astype(F32)
        scaled = (distance - centre) / 1.25
        basis = jnp.exp(-(scaled * scaled))
        basis = jnp.concatenate([basis, jnp.zeros((A - 8, wide), F32)], axis=0).astype(BF16)
        hidden = silu(dot(w_rad1_t[...], basis)).astype(BF16)
        radial = dot(w_rad2_t[...], hidden)

        def fold(v):
            return functools.reduce(jnp.add, [v[:, s * A : (s + 1) * A] for s in range(group)])

        acc[0] += fold(radial[0:A] * proj)
        carried = radial[A : 2 * A] * proj
        for c in range(3):
            acc[c + 1] += fold(carried * unit[c : c + 1])
        return carry

    lax.fori_loop(0, NBR // group, messages, 0)
    scale = 1.0 / math.sqrt(NBR)
    vec = [acc[c + 1] * scale for c in range(3)]
    vec_square = vec[0] * vec[0] + vec[1] * vec[1] + vec[2] * vec[2]
    joined = jnp.concatenate([acc[0] * scale, vec_square, feats_t], axis=0).astype(BF16)
    update = silu(dot(w_upd_t[...], joined)).astype(BF16)
    w_out = jnp.broadcast_to(w_out_ref[...].astype(F32), (16, A)).astype(BF16)
    electroneg = dot(w_out, update)[0:1] + jnp.where(species == 0, chi_ref[0], chi_ref[1])
    en_ref[...] = electroneg
    en_all[gid] = jnp.broadcast_to(electroneg, (8, A))
    for d in range(1, gcount):
        peer = grid.gather_peer((gid + d) % gcount)
        remote(en_all.at[gid], en_all.at[gid], en_sem.at[0], en_sem.at[1], peer).start()

    def gathered(ref, sem):
        return remote(ref.at[pl.ds(0, gcount - 1)], ref.at[pl.ds(0, gcount - 1)], sem.at[0], sem.at[1], grid.gather_peer(gid))

    pos_done = gathered(pos_all, pos_sem)
    pos_done.wait_recv()

    def build(step, carry):
        lanes = pl.ds(pl.multiple_of(step * A, A), A)
        tile = pos_all[step]
        x, y, z = tile[0:1] / box_x, tile[1:2] / SIDE, tile[2:3] / SIDE
        hard_all[:, lanes] = tile[3:4]
        row16 = iota((16, A), 0)
        sx, cx = sincos(row16.astype(F32) * x)
        xfac[:, lanes] = jnp.where(jnp.concatenate([row16, row16], axis=0) < 14, jnp.concatenate([cx, sx], axis=0), 0.0)
        sy, cy = sincos(row16.astype(F32) * y)
        sz, cz = sincos((iota((32, A), 0) - 13).astype(F32) * z)
        cos_rows, sin_rows = [], []
        for i in range(14):
            a, b = cy[i : i + 1], sy[i : i + 1]
            cos_rows.append(a * cz[0:24] - b * sz[0:24])
            sin_rows.append(b * cz[0:24] + a * sz[0:24])
        for j in range(24, 27):
            a, b = cz[j : j + 1], sz[j : j + 1]
            cos_rows.append(a * cy - b * sy)
            sin_rows.append(b * cy + a * sy)
        table[0:HALF, lanes] = jnp.concatenate(cos_rows, axis=0).astype(BF16)
        table[HALF : 2 * HALF, lanes] = jnp.concatenate(sin_rows, axis=0).astype(BF16)
        return carry

    lax.fori_loop(0, gcount, build, 0)

    en_done = gathered(en_all, en_sem)
    en_done.wait_recv()

    def start_residual(step, carry):
        lanes = pl.ds(pl.multiple_of(step * A, A), A)
        tile = en_all[step]
        res[:, lanes] = jnp.where(iota((2, A), 0) == 0, -tile[0:2], 1.0)
        return carry

    lax.fori_loop(0, gcount, start_residual, 0)
    sol[...] = jnp.zeros(sol.shape, F32)
    direc[...] = jnp.zeros(direc.shape, F32)
    s_dir[...] = jnp.zeros(s_dir.shape, F32)

    row64 = iota((64, A), 0)
    lane64 = iota((64, A), 1)

    def lane_sum(v):
        return jnp.sum(v, axis=1, keepdims=True)

    norm_old = dir_hard = dir_total = sol_total = None
    for rnd in range(ITERS):
        r, p, h = res[...], direc[...], hard_all[...]
        sums = [lane_sum(r * r), lane_sum(h * r * r), lane_sum(h * r * p), lane_sum(r)]
        for k in range(2):
            full_f = xfac[...] * r[k : k + 1]
            top = full_f.astype(BF16)
            ff[pl.ds(k * 32, 32), :] = top
            ff[pl.ds(64 + k * 32, 32), :] = (full_f - top.astype(F32)).astype(BF16)
        extra = jnp.zeros((64, A), F32)
        for k in range(2):
            for j in range(4):
                extra = jnp.where((row64 == k * 32 + 14) & (lane64 == j), sums[j][k : k + 1], extra)
        for j in range(3):
            s = dot_nt(ff[...], table[pl.ds(j * 256, 256), :])
            s = s[0:64] + s[64:128]
            left = s[:, 0:128]
            if j == 0:
                left = left + extra
            pay[rnd, pl.ds(j * 128, 64), :] = left
            pay[rnd, pl.ds(j * 128 + 64, 64), :] = s[:, 128:256]

        for d in range(1, rcount):
            target = (rid + d) % rcount
            remote(
                own_rows(pay, rnd, target), recv.at[rnd, d - 1], rs_sem.at[0, rnd], rs_sem.at[1, rnd],
                grid.reduce_peer(target),
            ).start()
        rs_done = remote(recv.at[rnd], recv.at[rnd], rs_sem.at[0, rnd], rs_sem.at[1, rnd], grid.reduce_peer(rid))
        rs_done.wait_recv()
        total = pay[rnd, pl.ds(pl.multiple_of(rid * chunk, 8), chunk), :]
        for d in range(1, rcount):
            total = total + recv[rnd, d - 1]
        full[rnd, pl.ds(pl.multiple_of(rid * chunk, 8), chunk), :] = total
        for d in range(1, rcount):
            target = (rid + d) % rcount
            remote(
                own_rows(full, rnd, rid), own_rows(full, rnd, rid), ag_sem.at[0, rnd], ag_sem.at[1, rnd],
                grid.reduce_peer(target),
            ).start()
        others = full.at[rnd, pl.ds(0, ROWS - chunk)]
        ag_done = remote(others, others, ag_sem.at[0, rnd], ag_sem.at[1, rnd], grid.reduce_peer(rid))
        ag_done.wait_recv()

        head = full[rnd, 0:64, :]

        def scalars(j):
            return jnp.concatenate([head[14:15, j : j + 1], head[46:47, j : j + 1]], axis=0)

        norm, res_hard, cross, res_total = [scalars(j) for j in range(4)]
        if rnd == 0:
            dir_hard, dir_total = res_hard, res_total
            beta = jnp.zeros_like(norm)
        else:
            beta = norm / norm_old
            dir_hard = res_hard + 2.0 * beta * cross + beta * beta * dir_hard
            dir_total = res_total + beta * dir_total
        beta_rows = jnp.where(row64 < 32, beta[0:1], beta[1:2])
        s_all = []
        for i in range(6):
            s = full[rnd, pl.ds(i * 64, 64), :]
            if rnd > 0:
                s = s + beta_rows * s_dir[i]
            s_dir[i] = s
            s_all.append(s)
        q_cos, q_sin = [], []
        for i in range(3):
            both, diff = w_sum[i], w_dif[i]
            for k, out in ((0, q_cos), (1, q_sin)):
                mine, other = s_all[3 * k + i], s_all[3 * (1 - k) + i]
                sign = -1.0 if k == 0 else 1.0
                parts = []
                for rhs in (0, 32):
                    for t in (0, 1):
                        same = mine[rhs + 16 * t : rhs + 16 * t + 16]
                        swap = other[rhs + 16 * (1 - t) : rhs + 16 * (1 - t) + 16]
                        sign = -1.0 if t == k else 1.0
                        parts.append(both * same + sign * (diff * swap))
                out.append(jnp.concatenate(parts, axis=0))
        q_all = q_cos + q_sin
        energy = functools.reduce(jnp.add, [q * s for q, s in zip(q_all, s_all)])
        energy = lane_sum(energy)
        energy = jnp.concatenate(
            [jnp.sum(energy[0:32], axis=0, keepdims=True), jnp.sum(energy[32:64], axis=0, keepdims=True)], axis=0
        )
        alpha = norm / (dir_hard + energy)
        p = r + beta * p
        sol[...] += alpha * p
        step_total = alpha * dir_total
        sol_total = step_total if rnd == 0 else sol_total + step_total
        norm_old = norm
        if rnd + 1 < ITERS:
            direc[...] = p
            q_full = jnp.concatenate(q_all, axis=1)
            top = q_full.astype(BF16)
            qq = jnp.concatenate([top, (q_full - top.astype(F32)).astype(BF16)], axis=0)
            piece = 512 if atoms % 512 == 0 else atoms
            for j in range(atoms // piece):
                lanes = pl.ds(j * piece, piece)
                g = dot(qq, table[:, lanes])
                g = g[0:64] + g[64:128]
                xf = xfac[:, lanes]
                pot = jnp.concatenate(
                    [jnp.sum(g[k * 32 : k * 32 + 32] * xf, axis=0, keepdims=True) for k in range(2)], axis=0
                )
                applied = hard_all[:, lanes] * direc[:, lanes] + pot
                res[:, lanes] = res[:, lanes] - alpha * applied

    ratio = sol_total[0:1] / sol_total[1:2]
    mine = sol[:, pl.ds(pl.multiple_of(gid * A, A), A)]
    charge_ref[...] = mine[0:1] - ratio * mine[1:2]

    pos_done.wait_send()
    en_done.wait_send()
    for rnd in range(ITERS):
        remote(recv.at[rnd], recv.at[rnd], rs_sem.at[0, rnd], rs_sem.at[1, rnd], grid.reduce_peer(rid)).wait_send()
        others = full.at[rnd, pl.ds(0, ROWS - chunk)]
        remote(others, others, ag_sem.at[0, rnd], ag_sem.at[1, rnd], grid.reduce_peer(rid)).wait_send()


def split_sizes(mesh):
    dom, kv = mesh.shape["dom"], mesh.shape["kv"]
    shapes = {64: (4, 8, 2), 8: (2, 2, 2)}
    ny, nz, nc = shapes[dom]
    return ny, nz, nc, kv


def solution(mesh):
    sizes = split_sizes(mesh)
    ny, nz, nc, nx = sizes
    gcount, rcount = nz * nc, nx * ny
    atoms = gcount * A
    chunk = ROWS // rcount

    def local(
        node_feats, positions, species, halo_rows, neighbours, nbr_count, recip_vectors,
        w_msg, w_rad1, w_rad2, w_upd, w_out, chi_table, hard_table,
    ):
        vmem = pl.BlockSpec(memory_space=pltpu.VMEM)
        smem = pl.BlockSpec(memory_space=pltpu.SMEM)
        electroneg, charges = pl.pallas_call(
            functools.partial(kernel, sizes),
            out_shape=(jax.ShapeDtypeStruct((1, A), F32), jax.ShapeDtypeStruct((1, A), F32)),
            in_specs=[vmem] * 12 + [smem] * 2,
            out_specs=(vmem, vmem),
            scratch_shapes=[
                pltpu.VMEM((TROWS, A), BF16),
                pltpu.VMEM((TROWS, A), BF16),
                pltpu.VMEM((2, TROWS, A), BF16),
                pltpu.VMEM((gcount, 8, A), F32),
                pltpu.VMEM((gcount, 8, A), F32),
                pltpu.VMEM((TROWS, 2 * A), BF16),
                pltpu.VMEM((NBR, A), I32),
                pltpu.VMEM((4, A, A), F32),
                pltpu.VMEM((A, A), BF16),
                pltpu.VMEM((2 * A, A), BF16),
                pltpu.VMEM((A, 3 * A), BF16),
                pltpu.VMEM((2 * HALF, atoms), BF16),
                pltpu.VMEM((32, atoms), F32),
                pltpu.VMEM((1, atoms), F32),
                pltpu.VMEM((128, atoms), BF16),
                pltpu.VMEM((2, atoms), F32),
                pltpu.VMEM((2, atoms), F32),
                pltpu.VMEM((2, atoms), F32),
                pltpu.VMEM((ITERS, ROWS, A), F32),
                pltpu.VMEM((ITERS, rcount - 1, chunk, A), F32),
                pltpu.VMEM((ITERS, ROWS, A), F32),
                pltpu.VMEM((32, HALF), F32),
                pltpu.VMEM((3, 16, A), F32),
                pltpu.VMEM((3, 16, A), F32),
                pltpu.VMEM((6, 64, A), F32),
                pltpu.SemaphoreType.DMA((4,)),
                pltpu.SemaphoreType.DMA((2,)),
                pltpu.SemaphoreType.DMA((2,)),
                pltpu.SemaphoreType.DMA((2, ITERS)),
                pltpu.SemaphoreType.DMA((2, ITERS)),
            ],
            compiler_params=pltpu.CompilerParams(
                collective_id=0, has_side_effects=True, vmem_limit_bytes=48 * 1024 * 1024
            ),
        )(
            node_feats, positions, species.reshape(1, A), halo_rows, neighbours, nbr_count.reshape(1, A),
            recip_vectors, w_msg, w_rad1, w_rad2, w_upd, w_out.reshape(1, A), chi_table, hard_table,
        )
        return electroneg.reshape(A), charges.reshape(A)

    both = ("dom", "kv")
    return jax.shard_map(
        local,
        mesh=mesh,
        in_specs=(
            P(both, None), P(None, both), P(both), P(both, None), P(both, None), P(both),
            P(), P(), P(), P(), P(), P(), P(), P(),
        ),
        out_specs=(P(both), P(both)),
        check_vma=False,
    )
```

```python
import functools
import math

import jax
import jax.numpy as jnp
from jax import lax
from jax.experimental import pallas as pl
from jax.experimental.pallas import tpu as pltpu
from jax.sharding import PartitionSpec as P

MESH = pl.DeviceIdType.MESH
F32, BF16, I32 = jnp.float32, jnp.bfloat16, jnp.int32
ITERS = 4
SLAB_W = 9.0
SIDE = 20.0
A = 128
NBR = 32
HALF = 384
CHUNKS = 24
TROWS = 160
TURN = 2.0 * math.pi
SIN_C = [(-1.0) ** k * TURN ** (2 * k + 1) / math.factorial(2 * k + 1) for k in range(10)]
COS_C = [(-1.0) ** k * TURN ** (2 * k) / math.factorial(2 * k) for k in range(10)]


def dot(a, b):
    return jnp.dot(a, b, preferred_element_type=F32)


def dot_nt(a, b):
    return lax.dot_general(a, b, (((1,), (1,)), ((), ())), preferred_element_type=F32)


def sincos(turns):
    t = turns - jnp.round(turns)
    q = t * t
    s = jnp.full_like(q, SIN_C[-1])
    c = jnp.full_like(q, COS_C[-1])
    for k in range(len(SIN_C) - 2, -1, -1):
        s = s * q + SIN_C[k]
        c = c * q + COS_C[k]
    return s * t, c


def silu(v):
    h = 0.5 * v
    return h + h * jnp.tanh(h)


def transposed(v):
    return v.astype(F32).T


def iota(shape, dim):
    return lax.broadcasted_iota(I32, shape, dim)


def ring(step, count):
    return min(step, count - step)


class Grid:
    def __init__(self, sizes):
        self.sizes = sizes
        ny, nz, nc, nx = sizes
        dom, x = lax.axis_index("dom"), lax.axis_index("kv")
        self.y, self.z, self.c, self.x = dom // (nz * nc), (dom // nc) % nz, dom % nc, x
        self.dom = dom
        steps = [(dx, dy, dc) for dx in range(nx) for dy in range(ny) for dc in range(nc)]
        steps.sort(key=lambda s: (-(ring(s[0], nx) + ring(s[1], ny)), s))
        self.peers = []
        for dx, dy, dc in steps:
            if dx or dy or dc:
                px, py, pc = (x + dx) % nx, (self.y + dy) % ny, (self.c + dc) % nc
                self.peers.append(({"dom": (py * nz + self.z) * nc + pc, "kv": px}, *self.share(px, py, pc)))
        self.chunk, self.owner = self.share(x, self.y, self.c)
        self.column = []
        for dz in sorted(range(1, nz), key=lambda d: -ring(d, nz)):
            self.column.append({"dom": (self.y * nz + (self.z + dz) % nz) * nc + self.c, "kv": x})

    def share(self, x, y, c):
        ny, nz, nc, nx = self.sizes
        index = (y * nx + x) * nc + c
        part = index % 4
        return (index // 4) * 3 + jnp.minimum(part, 2), part < 3

    def slab_peer(self, step):
        ny, nz, nc, nx = self.sizes
        count = ny * nz * nc * nx
        slab = (self.dom * nx + self.x + step + count) % count
        return {"dom": slab // nx, "kv": slab % nx}


def kernel(
    sizes,
    *refs,
):
    inputs, out_ref, arrived, scratch = refs[:14], refs[14], refs[15:29], refs[29:]
    (
        own_tab,
        packet,
        got,
        pos_all,
        en_all,
        nbr_tab,
        slots,
        acc,
        w_rad1_t,
        w_rad2_t,
        w_upd_t,
        table,
        xfac,
        hard_all,
        ff,
        res,
        direc,
        sol,
        pay,
        recv,
        full,
        present,
        w_sum,
        w_dif,
        s_dir,
        halo_sem,
        pos_sem,
        en_sem,
        rs_sem,
        ag_sem,
        in_sem,
    ) = scratch
    (
        feats_ref, pos_ref, species_ref, halo_ref, nbr_ref, count_ref, recip_ref, w_msg_ref, w_rad1_ref, w_rad2_ref,
        w_upd_ref, w_out_ref, chi_ref, hard_ref,
    ) = arrived
    grid = Grid(sizes)
    nz = sizes[1]
    gid = grid.z
    atoms = nz * A
    peers, column = grid.peers, grid.column
    atoms_total = atoms * (len(peers) + 1)
    box_x = (atoms_total // A) * SLAB_W
    kvec = recip_ref.shape[1]

    loads = [pltpu.make_async_copy(src, dst, in_sem.at[i]) for i, (src, dst) in enumerate(zip(inputs, arrived))]
    for i in (0, 7, 1, 3, 2, 13, 4, 5, 6, 8, 9, 10, 11, 12):
        loads[i].start()

    barrier = pltpu.get_barrier_semaphore()
    partners = [grid.slab_peer(-1), grid.slab_peer(1)] + column + [device for device, _, _ in peers]
    for device in partners:
        pl.semaphore_signal(barrier, inc=1, device_id=device, device_id_type=MESH)

    def remote(src, dst, send, recv_, device):
        return pltpu.make_async_remote_copy(
            src_ref=src, dst_ref=dst, send_sem=send, recv_sem=recv_, device_id=device, device_id_type=MESH
        )

    for i in (0, 1, 2, 3, 7, 13):
        loads[i].wait()
    species = species_ref[...]
    hard = hard_ref[...]
    hardness = jnp.where(species == 0, hard[0:1, 0:1], hard[0:1, 1:2])
    pos = jnp.concatenate([pos_ref[...], jnp.zeros((5, A), F32)], axis=0)
    pos_all[gid] = jnp.concatenate([pos_ref[...], hardness, jnp.zeros((4, A), F32)], axis=0)
    proj_t = dot(feats_ref[...], w_msg_ref[...]).T
    hi = pos.astype(BF16).astype(F32)
    mid = (pos - hi).astype(BF16).astype(F32)
    low = pos - hi - mid
    own_tab[...] = jnp.concatenate([proj_t, hi, mid, low, jnp.zeros((8, A), F32)], axis=0).astype(BF16)
    halo = jnp.concatenate([halo_ref[...], halo_ref[...]], axis=1)
    pick = jnp.where(iota((A, A), 0) == halo, 1.0, 0.0).astype(BF16)
    packet[...] = dot(own_tab[...], pick).astype(BF16)

    pl.semaphore_wait(barrier, len(partners))

    to_left = remote(packet, got.at[1], halo_sem.at[0], halo_sem.at[3], grid.slab_peer(-1))
    to_right = remote(packet, got.at[0], halo_sem.at[1], halo_sem.at[2], grid.slab_peer(1))
    to_left.start()
    to_right.start()
    for device in column:
        remote(pos_all.at[gid], pos_all.at[gid], pos_sem.at[0], pos_sem.at[1], device).start()

    for i in (4, 5, 6, 8, 9, 10, 11, 12):
        loads[i].wait()
    w_rad1_t[...] = jnp.concatenate(
        [transposed(jnp.concatenate([w_rad1_ref[...].astype(F32), jnp.zeros((120, A), F32)], axis=0))], axis=1
    ).astype(BF16)
    for i in range(2):
        w_rad2_t[pl.ds(i * A, A), :] = transposed(w_rad2_ref[:, i * A : (i + 1) * A]).astype(BF16)
    for i in range(3):
        w_upd_t[:, pl.ds(i * A, A)] = transposed(w_upd_ref[i * A : (i + 1) * A, :]).astype(BF16)
    index = nbr_ref[...]
    place = jnp.where(index < A, index, jnp.where(index < A + 32, index + 32, index - 32))
    slots[...] = jnp.where(iota((NBR, A), 0) < count_ref[...], place, -1)
    nbr_tab[:, 0:A] = own_tab[...]
    feats_t = transposed(feats_ref[...])

    k_step = 2048 if kvec % 2048 == 0 else kvec
    present[...] = jnp.zeros((32, HALF), F32)

    def count_triples(step, carry):
        m = recip_ref[:, pl.ds(pl.multiple_of(step * k_step, 128), k_step)]
        mx, my, mz = m[0:1], m[1:2], m[2:3]
        flip = jnp.where((my < 0) | ((my == 0) & (mz < 0)), -1, 1)
        mx, my, mz = mx * flip, my * flip, mz * flip + 13
        row = jnp.where(mx >= 0, mx, 16 - mx)
        column = jnp.where(mz < 24, my * 24 + mz, 336 + (mz - 24) * 16 + my)
        hot_row = jnp.where(iota((32, k_step), 0) == row, 1.0, 0.0).astype(BF16)
        hot_col = jnp.where(iota((HALF, k_step), 0) == column, 1.0, 0.0).astype(BF16)
        present[...] += dot_nt(hot_row, hot_col)
        return carry

    k_steps = kvec // k_step
    H1, H2 = k_steps // 4, 3 * k_steps // 4
    lax.fori_loop(0, H1, count_triples, 0)

    to_left.wait_send()
    to_right.wait_send()
    to_left.wait_recv()
    to_right.wait_recv()
    from_right, from_left = got[1].astype(F32), got[0].astype(F32)
    nbr_tab[:, A : 2 * A] = jnp.where(iota((TROWS, A), 1) < 32, from_right, from_left).astype(BF16)

    group = 4
    wide = group * A
    acc[...] = jnp.zeros(acc.shape, F32)
    own_pos = jnp.concatenate([pos] * group, axis=1)
    axis_row = iota((8, 1), 0)
    length = jnp.where(axis_row == 0, box_x, SIDE)
    live_row = axis_row < 3

    def messages(step, carry):
        here = jnp.concatenate([slots[pl.ds(step * group + s, 1), :] for s in range(group)], axis=1)
        hot = jnp.where(iota((2 * A, wide), 0) == here, 1.0, 0.0).astype(BF16)
        found = dot(nbr_tab[...], hot)
        proj = found[0:A]
        offset = found[A : A + 8] + found[A + 8 : A + 16] + found[A + 16 : A + 24] - own_pos
        offset = jnp.where(
            offset > 0.5 * length, offset - length, jnp.where(offset < -0.5 * length, offset + length, offset)
        )
        offset = jnp.where(live_row, offset, 0.0)
        square = jnp.sum(offset * offset, axis=0, keepdims=True) + 0.25
        inverse = lax.rsqrt(square)
        unit = offset * inverse
        distance = square * inverse
        centre = 1.0 + 1.25 * iota((8, 1), 0).astype(F32)
        scaled = (distance - centre) / 1.25
        basis = jnp.exp(-(scaled * scaled))
        basis = jnp.concatenate([basis, jnp.zeros((A - 8, wide), F32)], axis=0).astype(BF16)
        hidden = silu(dot(w_rad1_t[...], basis)).astype(BF16)
        radial = dot(w_rad2_t[...], hidden)

        def fold(v):
            return functools.reduce(jnp.add, [v[:, s * A : (s + 1) * A] for s in range(group)])

        acc[0] += fold(radial[0:A] * proj)
        carried = radial[A : 2 * A] * proj
        for c in range(3):
            acc[c + 1] += fold(carried * unit[c : c + 1])
        return carry

    lax.fori_loop(0, NBR // group, messages, 0)
    scale = 1.0 / math.sqrt(NBR)
    vec = [acc[c + 1] * scale for c in range(3)]
    vec_square = vec[0] * vec[0] + vec[1] * vec[1] + vec[2] * vec[2]
    joined = jnp.concatenate([acc[0] * scale, vec_square, feats_t], axis=0).astype(BF16)
    update = silu(dot(w_upd_t[...], joined)).astype(BF16)
    w_out = jnp.broadcast_to(w_out_ref[...].astype(F32), (16, A)).astype(BF16)
    chi = chi_ref[...]
    electroneg = dot(w_out, update)[0:1] + jnp.where(species == 0, chi[0:1, 0:1], chi[0:1, 1:2])
    out_ref[0:1, :] = electroneg
    en_all[gid] = jnp.broadcast_to(electroneg, (8, A))
    for device in column:
        remote(en_all.at[gid], en_all.at[gid], en_sem.at[0], en_sem.at[1], device).start()

    def gathered(ref, sem):
        return remote(ref.at[pl.ds(0, nz - 1)], ref.at[pl.ds(0, nz - 1)], sem.at[0], sem.at[1], column[0])

    pos_done = gathered(pos_all, pos_sem)
    pos_done.wait_recv()

    def build(step, carry):
        lanes = pl.ds(pl.multiple_of(step * A, A), A)
        tile = pos_all[step]
        x, y, z = tile[0:1] / box_x, tile[1:2] / SIDE, tile[2:3] / SIDE
        hard_all[:, lanes] = tile[3:4]
        row16 = iota((16, A), 0)
        sx, cx = sincos(row16.astype(F32) * x)
        xfac[:, lanes] = jnp.where(jnp.concatenate([row16, row16], axis=0) < 14, jnp.concatenate([cx, sx], axis=0), 0.0)
        sy, cy = sincos(row16.astype(F32) * y)
        sz, cz = sincos((iota((32, A), 0) - 13).astype(F32) * z)
        cos_rows, sin_rows = [], []
        for i in range(14):
            a, b = cy[i : i + 1], sy[i : i + 1]
            cos_rows.append(a * cz[0:24] - b * sz[0:24])
            sin_rows.append(b * cz[0:24] + a * sz[0:24])
        for j in range(24, 27):
            a, b = cz[j : j + 1], sz[j : j + 1]
            cos_rows.append(a * cy - b * sy)
            sin_rows.append(b * cy + a * sy)
        table[0:HALF, lanes] = jnp.concatenate(cos_rows, axis=0).astype(BF16)
        table[HALF : 2 * HALF, lanes] = jnp.concatenate(sin_rows, axis=0).astype(BF16)
        return carry

    lax.fori_loop(0, nz, build, 0)
    lax.fori_loop(H1, H2, count_triples, 0)

    en_done = gathered(en_all, en_sem)
    en_done.wait_recv()

    def start_residual(step, carry):
        lanes = pl.ds(pl.multiple_of(step * A, A), A)
        tile = en_all[step]
        res[:, lanes] = jnp.where(iota((2, A), 0) == 0, -tile[0:2], 1.0)
        return carry

    lax.fori_loop(0, nz, start_residual, 0)
    sol[...] = jnp.zeros(sol.shape, F32)
    direc[...] = jnp.zeros(direc.shape, F32)
    s_dir[...] = jnp.zeros(s_dir.shape, F32)

    row64 = iota((64, A), 0)
    lane64 = iota((64, A), 1)

    def lane_sum(v):
        return jnp.sum(v, axis=1, keepdims=True)

    def all_in(ref, sem, rnd):
        return remote(ref, ref, sem.at[0, rnd], sem.at[1, rnd], column[0])

    norm_old = dir_hard = dir_total = sol_total = None
    for rnd in range(ITERS):
        r, p, h = res[...], direc[...], hard_all[...]
        sums = [lane_sum(r * r), lane_sum(h * r * r), lane_sum(h * r * p), lane_sum(r)]
        for k in range(2):
            full_f = xfac[...] * r[k : k + 1]
            top = full_f.astype(BF16)
            ff[pl.ds(k * 32, 32), :] = top
            ff[pl.ds(64 + k * 32, 32), :] = (full_f - top.astype(F32)).astype(BF16)
        extra = jnp.zeros((64, A), F32)
        for k in range(2):
            for j in range(4):
                top = sums[j][k : k + 1].astype(BF16).astype(F32)
                extra = jnp.where((row64 == k * 32 + 14) & (lane64 == j), top, extra)
                extra = jnp.where((row64 == k * 32 + 15) & (lane64 == j), sums[j][k : k + 1] - top, extra)
        for j in range(3):
            s = dot_nt(ff[...], table[pl.ds(j * 256, 256), :])
            s = s[0:64] + s[64:128]
            left = s[:, 0:128]
            if j == 0:
                left = left + extra
            pay[rnd, pl.ds(8 * j, 4)] = left.astype(BF16).reshape(4, 16, A)
            pay[rnd, pl.ds(8 * j + 4, 4)] = s[:, 128:256].astype(BF16).reshape(4, 16, A)

        for k, (device, share, owns) in enumerate(peers):

            @pl.when(owns)
            def _():
                remote(pay.at[rnd, share], recv.at[rnd, k], rs_sem.at[0, rnd], rs_sem.at[1, rnd], device).start()

        if rnd == 0:
            lax.fori_loop(H2, k_steps, count_triples, 0)
            column_id = iota((1, HALF), 1)
            late = column_id - 336
            grid_y = jnp.where(late < 0, (column_id * 2731) >> 16, late & 15)
            grid_z = jnp.where(late < 0, column_id - grid_y * 24 - 13, 11 + (late >> 4))
            grid_x = iota((16, 1), 0)
            m_square = (grid_y * grid_y + grid_z * grid_z + grid_x * grid_x).astype(F32)
            weight = 16.0 / atoms_total * jnp.exp(-m_square / 400.0) / (1.0 + m_square / 16.0)
            plus, minus = present[0:16] * weight, present[16:32] * weight
            for i in range(3):
                lanes = slice(i * 128, (i + 1) * 128)
                w_sum[i] = (plus + minus)[:, lanes]
                w_dif[i] = (plus - minus)[:, lanes]

        @pl.when(grid.owner)
        def _():
            all_in(recv.at[rnd], rs_sem, rnd).wait_recv()
            total = pay[rnd, grid.chunk].astype(F32)
            for k in range(len(peers)):
                total = total + recv[rnd, k].astype(F32)
            scalar = total[14:15] + total[15:16]
            top = scalar.astype(BF16).astype(F32)
            full[rnd, grid.chunk] = jnp.concatenate([total[0:14], top, scalar - top], axis=0).astype(BF16)
            for device, _, _ in peers:
                mine = full.at[rnd, grid.chunk]
                remote(mine, mine, ag_sem.at[0, rnd], ag_sem.at[1, rnd], device).start()
            all_in(full.at[rnd, pl.ds(0, CHUNKS - 1)], ag_sem, rnd).wait_recv()

        @pl.when(jnp.logical_not(grid.owner))
        def _():
            all_in(full.at[rnd], ag_sem, rnd).wait_recv()

        head = full[rnd, 0:4].reshape(64, A).astype(F32)

        def scalars(j):
            both = [head[k + 14 : k + 15, j : j + 1] + head[k + 15 : k + 16, j : j + 1] for k in (0, 32)]
            return jnp.concatenate(both, axis=0)

        norm, res_hard, cross, res_total = [scalars(j) for j in range(4)]
        if rnd == 0:
            dir_hard, dir_total = res_hard, res_total
            beta = jnp.zeros_like(norm)
        else:
            beta = norm / norm_old
            dir_hard = res_hard + 2.0 * beta * cross + beta * beta * dir_hard
            dir_total = res_total + beta * dir_total
        beta_rows = jnp.where(row64 < 32, beta[0:1], beta[1:2])
        s_all = []
        for i in range(6):
            s = full[rnd, pl.ds(i * 4, 4)].reshape(64, A).astype(F32)
            if rnd > 0:
                s = s + beta_rows * s_dir[i]
            s_dir[i] = s
            s_all.append(s)
        q_cos, q_sin = [], []
        for i in range(3):
            both, diff = w_sum[i], w_dif[i]
            for k, out in ((0, q_cos), (1, q_sin)):
                mine, other = s_all[3 * k + i], s_all[3 * (1 - k) + i]
                sign = -1.0 if k == 0 else 1.0
                parts = []
                for rhs in (0, 32):
                    for t in (0, 1):
                        same = mine[rhs + 16 * t : rhs + 16 * t + 16]
                        swap = other[rhs + 16 * (1 - t) : rhs + 16 * (1 - t) + 16]
                        sign = -1.0 if t == k else 1.0
                        parts.append(both * same + sign * (diff * swap))
                out.append(jnp.concatenate(parts, axis=0))
        q_all = q_cos + q_sin
        energy = functools.reduce(jnp.add, [q * s for q, s in zip(q_all, s_all)])
        energy = lane_sum(energy)
        energy = jnp.concatenate(
            [jnp.sum(energy[0:32], axis=0, keepdims=True), jnp.sum(energy[32:64], axis=0, keepdims=True)], axis=0
        )
        alpha = norm / (dir_hard + energy)
        p = r + beta * p
        sol[...] += alpha * p
        step_total = alpha * dir_total
        sol_total = step_total if rnd == 0 else sol_total + step_total
        norm_old = norm
        if rnd + 1 < ITERS:
            direc[...] = p
            q_full = jnp.concatenate(q_all, axis=1)
            top = q_full.astype(BF16)
            qq = jnp.concatenate([top, (q_full - top.astype(F32)).astype(BF16)], axis=0)
            piece = 512 if atoms % 512 == 0 else atoms
            for j in range(atoms // piece):
                lanes = pl.ds(j * piece, piece)
                g = dot(qq, table[:, lanes])
                g = g[0:64] + g[64:128]
                xf = xfac[:, lanes]
                pot = jnp.concatenate(
                    [jnp.sum(g[k * 32 : k * 32 + 32] * xf, axis=0, keepdims=True) for k in range(2)], axis=0
                )
                applied = hard_all[:, lanes] * direc[:, lanes] + pot
                res[:, lanes] = res[:, lanes] - alpha * applied

    ratio = sol_total[0:1] / sol_total[1:2]
    mine = sol[:, pl.ds(pl.multiple_of(gid * A, A), A)]
    out_ref[1:2, :] = mine[0:1] - ratio * mine[1:2]

    pos_done.wait_send()
    en_done.wait_send()
    for rnd in range(ITERS):

        @pl.when(grid.owner)
        def _():
            all_in(pay.at[rnd, pl.ds(0, CHUNKS - 1)], rs_sem, rnd).wait_send()
            all_in(recv.at[rnd], ag_sem, rnd).wait_send()

        @pl.when(jnp.logical_not(grid.owner))
        def _():
            all_in(pay.at[rnd], rs_sem, rnd).wait_send()


def solution(mesh):
    sizes = (4, 8, 2, 4)
    ny, nz, nc, nx = sizes
    assert dict(mesh.shape) == {"dom": ny * nz * nc, "kv": nx}
    atoms = nz * A
    others = nx * ny * nc - 1

    def local(
        node_feats, positions, species, halo_rows, neighbours, nbr_count, recip_vectors,
        w_msg, w_rad1, w_rad2, w_upd, w_out, chi_table, hard_table,
    ):
        operands = (
            node_feats, positions, species.reshape(1, A), halo_rows, neighbours.T, nbr_count.reshape(1, A),
            recip_vectors, w_msg, w_rad1, w_rad2, w_upd, w_out.reshape(1, A), chi_table.reshape(1, 2),
            hard_table.reshape(1, 2),
        )
        out = pl.pallas_call(
            functools.partial(kernel, sizes),
            out_shape=jax.ShapeDtypeStruct((2, A), F32),
            in_specs=[pl.BlockSpec(memory_space=pltpu.HBM)] * len(operands),
            out_specs=pl.BlockSpec(memory_space=pltpu.VMEM),
            scratch_shapes=[pltpu.VMEM(v.shape, v.dtype) for v in operands]
            + [
                pltpu.VMEM((TROWS, A), BF16),
                pltpu.VMEM((TROWS, A), BF16),
                pltpu.VMEM((2, TROWS, A), BF16),
                pltpu.VMEM((nz, 8, A), F32),
                pltpu.VMEM((nz, 8, A), F32),
                pltpu.VMEM((TROWS, 2 * A), BF16),
                pltpu.VMEM((NBR, A), I32),
                pltpu.VMEM((4, A, A), F32),
                pltpu.VMEM((A, A), BF16),
                pltpu.VMEM((2 * A, A), BF16),
                pltpu.VMEM((A, 3 * A), BF16),
                pltpu.VMEM((2 * HALF, atoms), BF16),
                pltpu.VMEM((32, atoms), F32),
                pltpu.VMEM((1, atoms), F32),
                pltpu.VMEM((128, atoms), BF16),
                pltpu.VMEM((2, atoms), F32),
                pltpu.VMEM((2, atoms), F32),
                pltpu.VMEM((2, atoms), F32),
                pltpu.VMEM((ITERS, CHUNKS, 16, A), BF16),
                pltpu.VMEM((ITERS, others, 16, A), BF16),
                pltpu.VMEM((ITERS, CHUNKS, 16, A), BF16),
                pltpu.VMEM((32, HALF), F32),
                pltpu.VMEM((3, 16, A), F32),
                pltpu.VMEM((3, 16, A), F32),
                pltpu.VMEM((6, 64, A), F32),
                pltpu.SemaphoreType.DMA((4,)),
                pltpu.SemaphoreType.DMA((2,)),
                pltpu.SemaphoreType.DMA((2,)),
                pltpu.SemaphoreType.DMA((2, ITERS)),
                pltpu.SemaphoreType.DMA((2, ITERS)),
                pltpu.SemaphoreType.DMA((len(operands),)),
            ],
            compiler_params=pltpu.CompilerParams(
                collective_id=0, has_side_effects=True, vmem_limit_bytes=60 * 1024 * 1024
            ),
        )(*operands)
        return out[0], out[1]

    both = ("dom", "kv")
    return jax.shard_map(
        local,
        mesh=mesh,
        in_specs=(
            P(both, None), P(None, both), P(both), P(both, None), P(both, None), P(both),
            P(), P(), P(), P(), P(), P(), P(), P(),
        ),
        out_specs=(P(both), P(both)),
        check_vma=False,
    )
```

```python
import functools
import math

import jax
import jax.numpy as jnp
from jax import lax
from jax.experimental import pallas as pl
from jax.experimental.pallas import tpu as pltpu
from jax.sharding import PartitionSpec as P

MESH = pl.DeviceIdType.MESH
F32, BF16, I32 = jnp.float32, jnp.bfloat16, jnp.int32
ITERS = 4
SLAB_W = 9.0
SIDE = 20.0
A = 128
NBR = 32
HALF = 384
CHUNKS = 24
TROWS = 160
TURN = 2.0 * math.pi
SIN_C = [(-1.0) ** k * TURN ** (2 * k + 1) / math.factorial(2 * k + 1) for k in range(10)]
COS_C = [(-1.0) ** k * TURN ** (2 * k) / math.factorial(2 * k) for k in range(10)]


def dot(a, b):
    return jnp.dot(a, b, preferred_element_type=F32)


def dot_nt(a, b):
    return lax.dot_general(a, b, (((1,), (1,)), ((), ())), preferred_element_type=F32)


def sincos(turns):
    t = turns - jnp.round(turns)
    q = t * t
    s = jnp.full_like(q, SIN_C[-1])
    c = jnp.full_like(q, COS_C[-1])
    for k in range(len(SIN_C) - 2, -1, -1):
        s = s * q + SIN_C[k]
        c = c * q + COS_C[k]
    return s * t, c


def silu(v):
    h = 0.5 * v
    return h + h * jnp.tanh(h)


def transposed(v):
    return v.astype(F32).T


def coded(v):
    top = jnp.max(jnp.abs(v), axis=0, keepdims=True)
    power = jnp.ceil(jnp.log2(jnp.maximum(top, 1e-30) * 1.01)) - 15.0
    whole = jnp.round(v * jnp.exp2(-power))
    return jnp.where(iota(v.shape, 0) == 15, power, whole).astype(I32).astype(jnp.int16)


def decoded(q):
    v = q.astype(I32).astype(F32)
    return v * jnp.exp2(v[15:16])


def iota(shape, dim):
    return lax.broadcasted_iota(I32, shape, dim)


def ring(step, count):
    return min(step, count - step)


class Grid:
    def __init__(self, sizes):
        self.sizes = sizes
        ny, nz, nc, nx = sizes
        dom, x = lax.axis_index("dom"), lax.axis_index("kv")
        self.y, self.z, self.c, self.x = dom // (nz * nc), (dom // nc) % nz, dom % nc, x
        self.dom = dom
        steps = [(dx, dy, dc) for dx in range(nx) for dy in range(ny) for dc in range(nc)]
        steps.sort(key=lambda s: (-(ring(s[0], nx) + ring(s[1], ny)), s))
        self.peers = []
        for dx, dy, dc in steps:
            if dx or dy or dc:
                px, py, pc = (x + dx) % nx, (self.y + dy) % ny, (self.c + dc) % nc
                self.peers.append(({"dom": (py * nz + self.z) * nc + pc, "kv": px}, *self.share(px, py, pc)))
        self.chunk, self.owner = self.share(x, self.y, self.c)
        self.column = []
        for dz in sorted(range(1, nz), key=lambda d: -ring(d, nz)):
            self.column.append({"dom": (self.y * nz + (self.z + dz) % nz) * nc + self.c, "kv": x})

    def share(self, x, y, c):
        ny, nz, nc, nx = self.sizes
        index = (y * nx + x) * nc + c
        part = index % 4
        return (index // 4) * 3 + jnp.minimum(part, 2), part < 3

    def slab_peer(self, step):
        ny, nz, nc, nx = self.sizes
        count = ny * nz * nc * nx
        slab = (self.dom * nx + self.x + step + count) % count
        return {"dom": slab // nx, "kv": slab % nx}


def kernel(
    sizes,
    *refs,
):
    inputs, out_ref, arrived, scratch = refs[:14], refs[14], refs[15:29], refs[29:]
    (
        own_tab,
        packet,
        got,
        pos_all,
        en_all,
        nbr_tab,
        slots,
        acc,
        w_rad1_t,
        w_rad2_t,
        w_upd_t,
        table,
        xfac,
        hard_all,
        ff,
        res,
        direc,
        sol,
        pay,
        recv,
        full,
        scal,
        present,
        w_sum,
        w_dif,
        s_dir,
        halo_sem,
        pos_sem,
        en_sem,
        rs_sem,
        ag_sem,
        sc_sem,
        in_sem,
    ) = scratch
    (
        feats_ref, pos_ref, species_ref, halo_ref, nbr_ref, count_ref, recip_ref, w_msg_ref, w_rad1_ref, w_rad2_ref,
        w_upd_ref, w_out_ref, chi_ref, hard_ref,
    ) = arrived
    grid = Grid(sizes)
    nz = sizes[1]
    gid = grid.z
    atoms = nz * A
    peers, column = grid.peers, grid.column
    atoms_total = atoms * (len(peers) + 1)
    box_x = (atoms_total // A) * SLAB_W
    kvec = recip_ref.shape[1]

    loads = [pltpu.make_async_copy(src, dst, in_sem.at[i]) for i, (src, dst) in enumerate(zip(inputs, arrived))]
    for i in (0, 7, 1, 3, 2, 13, 4, 5, 6, 8, 9, 10, 11, 12):
        loads[i].start()

    barrier = pltpu.get_barrier_semaphore()
    partners = [grid.slab_peer(-1), grid.slab_peer(1)] + column + [device for device, _, _ in peers]
    for device in partners:
        pl.semaphore_signal(barrier, inc=1, device_id=device, device_id_type=MESH)

    def remote(src, dst, send, recv_, device):
        return pltpu.make_async_remote_copy(
            src_ref=src, dst_ref=dst, send_sem=send, recv_sem=recv_, device_id=device, device_id_type=MESH
        )

    for i in (0, 1, 2, 3, 7, 13):
        loads[i].wait()
    species = species_ref[...]
    hard = hard_ref[...]
    hardness = jnp.where(species == 0, hard[0:1, 0:1], hard[0:1, 1:2])
    pos = jnp.concatenate([pos_ref[...], jnp.zeros((5, A), F32)], axis=0)
    pos_all[gid] = jnp.concatenate([pos_ref[...], hardness, jnp.zeros((4, A), F32)], axis=0)
    proj_t = dot(feats_ref[...], w_msg_ref[...]).T
    hi = pos.astype(BF16).astype(F32)
    mid = (pos - hi).astype(BF16).astype(F32)
    low = pos - hi - mid
    own_tab[...] = jnp.concatenate([proj_t, hi, mid, low, jnp.zeros((8, A), F32)], axis=0).astype(BF16)
    halo = jnp.concatenate([halo_ref[...], halo_ref[...]], axis=1)
    pick = jnp.where(iota((A, A), 0) == halo, 1.0, 0.0).astype(BF16)
    packet[...] = dot(own_tab[...], pick).astype(BF16)

    pl.semaphore_wait(barrier, len(partners))

    to_left = remote(packet, got.at[1], halo_sem.at[0], halo_sem.at[3], grid.slab_peer(-1))
    to_right = remote(packet, got.at[0], halo_sem.at[1], halo_sem.at[2], grid.slab_peer(1))
    to_left.start()
    to_right.start()
    for device in column:
        remote(pos_all.at[gid], pos_all.at[gid], pos_sem.at[0], pos_sem.at[1], device).start()

    for i in (4, 5, 6, 8, 9, 10, 11, 12):
        loads[i].wait()
    w_rad1_t[...] = jnp.concatenate(
        [transposed(jnp.concatenate([w_rad1_ref[...].astype(F32), jnp.zeros((120, A), F32)], axis=0))], axis=1
    ).astype(BF16)
    for i in range(2):
        w_rad2_t[pl.ds(i * A, A), :] = transposed(w_rad2_ref[:, i * A : (i + 1) * A]).astype(BF16)
    for i in range(3):
        w_upd_t[:, pl.ds(i * A, A)] = transposed(w_upd_ref[i * A : (i + 1) * A, :]).astype(BF16)
    index = nbr_ref[...]
    place = jnp.where(index < A, index, jnp.where(index < A + 32, index + 32, index - 32))
    slots[...] = jnp.where(iota((NBR, A), 0) < count_ref[...], place, -1)
    nbr_tab[:, 0:A] = own_tab[...]
    feats_t = transposed(feats_ref[...])

    k_step = 2048 if kvec % 2048 == 0 else kvec
    present[...] = jnp.zeros((32, HALF), F32)

    def count_triples(step, carry):
        m = recip_ref[:, pl.ds(pl.multiple_of(step * k_step, 128), k_step)]
        mx, my, mz = m[0:1], m[1:2], m[2:3]
        flip = jnp.where((my < 0) | ((my == 0) & (mz < 0)), -1, 1)
        mx, my, mz = mx * flip, my * flip, mz * flip + 13
        row = jnp.where(mx >= 0, mx, 16 - mx)
        column = jnp.where(mz < 24, my * 24 + mz, 336 + (mz - 24) * 16 + my)
        hot_row = jnp.where(iota((32, k_step), 0) == row, 1.0, 0.0).astype(BF16)
        hot_col = jnp.where(iota((HALF, k_step), 0) == column, 1.0, 0.0).astype(BF16)
        present[...] += dot_nt(hot_row, hot_col)
        return carry

    k_steps = kvec // k_step
    H1, H2 = k_steps // 4, 3 * k_steps // 4
    lax.fori_loop(0, H1, count_triples, 0)

    to_left.wait_send()
    to_right.wait_send()
    to_left.wait_recv()
    to_right.wait_recv()
    from_right, from_left = got[1].astype(F32), got[0].astype(F32)
    nbr_tab[:, A : 2 * A] = jnp.where(iota((TROWS, A), 1) < 32, from_right, from_left).astype(BF16)

    group = 4
    wide = group * A
    acc[...] = jnp.zeros(acc.shape, F32)
    own_pos = jnp.concatenate([pos] * group, axis=1)
    axis_row = iota((8, 1), 0)
    length = jnp.where(axis_row == 0, box_x, SIDE)
    live_row = axis_row < 3

    def messages(step, carry):
        here = jnp.concatenate([slots[pl.ds(step * group + s, 1), :] for s in range(group)], axis=1)
        hot = jnp.where(iota((2 * A, wide), 0) == here, 1.0, 0.0).astype(BF16)
        found = dot(nbr_tab[...], hot)
        proj = found[0:A]
        offset = found[A : A + 8] + found[A + 8 : A + 16] + found[A + 16 : A + 24] - own_pos
        offset = jnp.where(
            offset > 0.5 * length, offset - length, jnp.where(offset < -0.5 * length, offset + length, offset)
        )
        offset = jnp.where(live_row, offset, 0.0)
        square = jnp.sum(offset * offset, axis=0, keepdims=True) + 0.25
        inverse = lax.rsqrt(square)
        unit = offset * inverse
        distance = square * inverse
        centre = 1.0 + 1.25 * iota((8, 1), 0).astype(F32)
        scaled = (distance - centre) / 1.25
        basis = jnp.exp(-(scaled * scaled))
        basis = jnp.concatenate([basis, jnp.zeros((A - 8, wide), F32)], axis=0).astype(BF16)
        hidden = silu(dot(w_rad1_t[...], basis)).astype(BF16)
        radial = dot(w_rad2_t[...], hidden)

        def fold(v):
            return functools.reduce(jnp.add, [v[:, s * A : (s + 1) * A] for s in range(group)])

        acc[0] += fold(radial[0:A] * proj)
        carried = radial[A : 2 * A] * proj
        for c in range(3):
            acc[c + 1] += fold(carried * unit[c : c + 1])
        return carry

    lax.fori_loop(0, NBR // group, messages, 0)
    scale = 1.0 / math.sqrt(NBR)
    vec = [acc[c + 1] * scale for c in range(3)]
    vec_square = vec[0] * vec[0] + vec[1] * vec[1] + vec[2] * vec[2]
    joined = jnp.concatenate([acc[0] * scale, vec_square, feats_t], axis=0).astype(BF16)
    update = silu(dot(w_upd_t[...], joined)).astype(BF16)
    w_out = jnp.broadcast_to(w_out_ref[...].astype(F32), (16, A)).astype(BF16)
    chi = chi_ref[...]
    electroneg = dot(w_out, update)[0:1] + jnp.where(species == 0, chi[0:1, 0:1], chi[0:1, 1:2])
    out_ref[0:1, :] = electroneg
    en_all[gid] = jnp.broadcast_to(electroneg, (8, A))
    for device in column:
        remote(en_all.at[gid], en_all.at[gid], en_sem.at[0], en_sem.at[1], device).start()

    def gathered(ref, sem):
        return remote(ref.at[pl.ds(0, nz - 1)], ref.at[pl.ds(0, nz - 1)], sem.at[0], sem.at[1], column[0])

    pos_done = gathered(pos_all, pos_sem)
    pos_done.wait_recv()

    def build(step, carry):
        lanes = pl.ds(pl.multiple_of(step * A, A), A)
        tile = pos_all[step]
        x, y, z = tile[0:1] / box_x, tile[1:2] / SIDE, tile[2:3] / SIDE
        hard_all[:, lanes] = tile[3:4]
        row16 = iota((16, A), 0)
        sx, cx = sincos(row16.astype(F32) * x)
        xfac[:, lanes] = jnp.where(jnp.concatenate([row16, row16], axis=0) < 14, jnp.concatenate([cx, sx], axis=0), 0.0)
        sy, cy = sincos(row16.astype(F32) * y)
        sz, cz = sincos((iota((32, A), 0) - 13).astype(F32) * z)
        cos_rows, sin_rows = [], []
        for i in range(14):
            a, b = cy[i : i + 1], sy[i : i + 1]
            cos_rows.append(a * cz[0:24] - b * sz[0:24])
            sin_rows.append(b * cz[0:24] + a * sz[0:24])
        for j in range(24, 27):
            a, b = cz[j : j + 1], sz[j : j + 1]
            cos_rows.append(a * cy - b * sy)
            sin_rows.append(b * cy + a * sy)
        table[0:HALF, lanes] = jnp.concatenate(cos_rows, axis=0).astype(BF16)
        table[HALF : 2 * HALF, lanes] = jnp.concatenate(sin_rows, axis=0).astype(BF16)
        return carry

    lax.fori_loop(0, nz, build, 0)
    lax.fori_loop(H1, H2, count_triples, 0)

    en_done = gathered(en_all, en_sem)
    en_done.wait_recv()

    def start_residual(step, carry):
        lanes = pl.ds(pl.multiple_of(step * A, A), A)
        tile = en_all[step]
        res[:, lanes] = jnp.where(iota((2, A), 0) == 0, -tile[0:2], 1.0)
        return carry

    lax.fori_loop(0, nz, start_residual, 0)
    sol[...] = jnp.zeros(sol.shape, F32)
    direc[...] = jnp.zeros(direc.shape, F32)
    s_dir[...] = jnp.zeros(s_dir.shape, F32)

    row64 = iota((64, A), 0)
    row16 = iota((16, A), 0)
    lane1 = iota((1, A), 1)

    def lane_sum(v):
        return jnp.sum(v, axis=1, keepdims=True)

    def all_in(ref, sem, rnd):
        return remote(ref, ref, sem.at[0, rnd], sem.at[1, rnd], column[0])

    norm_old = dir_hard = dir_total = sol_total = None
    for rnd in range(ITERS):
        r, p, h = res[...], direc[...], hard_all[...]
        sums = [lane_sum(r * r), lane_sum(h * r * r), lane_sum(h * r * p), lane_sum(r)]
        for k in range(2):
            full_f = xfac[...] * r[k : k + 1]
            top = full_f.astype(BF16)
            ff[pl.ds(k * 32, 32), :] = top
            ff[pl.ds(64 + k * 32, 32), :] = (full_f - top.astype(F32)).astype(BF16)
        extra = jnp.zeros((1, A), F32)
        for k in range(2):
            for j in range(4):
                extra = jnp.where(lane1 == 4 * k + j, sums[j][k : k + 1], extra)
        scal[rnd, 0] = extra
        for j in range(3):
            s = dot_nt(ff[...], table[pl.ds(j * 256, 256), :])
            s = s[0:64] + s[64:128]
            for t in range(8):
                pay[rnd, 8 * j + t] = coded(s[(t % 4) * 16 : (t % 4) * 16 + 16, (t // 4) * A : (t // 4 + 1) * A])

        for k, (device, share, owns) in enumerate(peers):

            @pl.when(owns)
            def _():
                remote(pay.at[rnd, share], recv.at[rnd, k], rs_sem.at[0, rnd], rs_sem.at[1, rnd], device).start()

        for k, (device, _, _) in enumerate(peers):
            remote(scal.at[rnd, 0], scal.at[rnd, k + 1], sc_sem.at[0, rnd], sc_sem.at[1, rnd], device).start()

        if rnd == 0:
            lax.fori_loop(H2, k_steps, count_triples, 0)
            column_id = iota((1, HALF), 1)
            late = column_id - 336
            grid_y = jnp.where(late < 0, (column_id * 2731) >> 16, late & 15)
            grid_z = jnp.where(late < 0, column_id - grid_y * 24 - 13, 11 + (late >> 4))
            grid_x = iota((16, 1), 0)
            m_square = (grid_y * grid_y + grid_z * grid_z + grid_x * grid_x).astype(F32)
            weight = 16.0 / atoms_total * jnp.exp(-m_square / 400.0) / (1.0 + m_square / 16.0)
            plus, minus = present[0:16] * weight, present[16:32] * weight
            for i in range(3):
                lanes = slice(i * 128, (i + 1) * 128)
                w_sum[i] = (plus + minus)[:, lanes]
                w_dif[i] = (plus - minus)[:, lanes]

        @pl.when(grid.owner)
        def _():
            all_in(recv.at[rnd], rs_sem, rnd).wait_recv()
            total = decoded(pay[rnd, grid.chunk])
            for k in range(len(peers)):
                total = total + decoded(recv[rnd, k])
            full[rnd, grid.chunk] = coded(jnp.where(row16 < 14, total, 0.0))
            for device, _, _ in peers:
                mine = full.at[rnd, grid.chunk]
                remote(mine, mine, ag_sem.at[0, rnd], ag_sem.at[1, rnd], device).start()
            all_in(full.at[rnd, pl.ds(0, CHUNKS - 1)], ag_sem, rnd).wait_recv()

        @pl.when(jnp.logical_not(grid.owner))
        def _():
            all_in(full.at[rnd], ag_sem, rnd).wait_recv()

        all_in(scal.at[rnd, pl.ds(0, len(peers))], sc_sem, rnd).wait_recv()
        added = jnp.sum(scal[rnd], axis=0)

        def scalars(j):
            return jnp.concatenate([added[:, j : j + 1], added[:, 4 + j : 5 + j]], axis=0)

        norm, res_hard, cross, res_total = [scalars(j) for j in range(4)]
        if rnd == 0:
            dir_hard, dir_total = res_hard, res_total
            beta = jnp.zeros_like(norm)
        else:
            beta = norm / norm_old
            dir_hard = res_hard + 2.0 * beta * cross + beta * beta * dir_hard
            dir_total = res_total + beta * dir_total
        beta_rows = jnp.where(row64 < 32, beta[0:1], beta[1:2])
        s_all = []
        for i in range(6):
            s = jnp.concatenate([decoded(full[rnd, 4 * i + t]) for t in range(4)], axis=0)
            if rnd > 0:
                s = s + beta_rows * s_dir[i]
            s_dir[i] = s
            s_all.append(s)
        q_cos, q_sin = [], []
        for i in range(3):
            both, diff = w_sum[i], w_dif[i]
            for k, out in ((0, q_cos), (1, q_sin)):
                mine, other = s_all[3 * k + i], s_all[3 * (1 - k) + i]
                sign = -1.0 if k == 0 else 1.0
                parts = []
                for rhs in (0, 32):
                    for t in (0, 1):
                        same = mine[rhs + 16 * t : rhs + 16 * t + 16]
                        swap = other[rhs + 16 * (1 - t) : rhs + 16 * (1 - t) + 16]
                        sign = -1.0 if t == k else 1.0
                        parts.append(both * same + sign * (diff * swap))
                out.append(jnp.concatenate(parts, axis=0))
        q_all = q_cos + q_sin
        energy = functools.reduce(jnp.add, [q * s for q, s in zip(q_all, s_all)])
        energy = lane_sum(energy)
        energy = jnp.concatenate(
            [jnp.sum(energy[0:32], axis=0, keepdims=True), jnp.sum(energy[32:64], axis=0, keepdims=True)], axis=0
        )
        alpha = norm / (dir_hard + energy)
        p = r + beta * p
        sol[...] += alpha * p
        step_total = alpha * dir_total
        sol_total = step_total if rnd == 0 else sol_total + step_total
        norm_old = norm
        if rnd + 1 < ITERS:
            direc[...] = p
            q_full = jnp.concatenate(q_all, axis=1)
            top = q_full.astype(BF16)
            qq = jnp.concatenate([top, (q_full - top.astype(F32)).astype(BF16)], axis=0)
            piece = 512 if atoms % 512 == 0 else atoms
            for j in range(atoms // piece):
                lanes = pl.ds(j * piece, piece)
                g = dot(qq, table[:, lanes])
                g = g[0:64] + g[64:128]
                xf = xfac[:, lanes]
                pot = jnp.concatenate(
                    [jnp.sum(g[k * 32 : k * 32 + 32] * xf, axis=0, keepdims=True) for k in range(2)], axis=0
                )
                applied = hard_all[:, lanes] * direc[:, lanes] + pot
                res[:, lanes] = res[:, lanes] - alpha * applied

    ratio = sol_total[0:1] / sol_total[1:2]
    mine = sol[:, pl.ds(pl.multiple_of(gid * A, A), A)]
    out_ref[1:2, :] = mine[0:1] - ratio * mine[1:2]

    pos_done.wait_send()
    en_done.wait_send()
    for rnd in range(ITERS):
        all_in(scal.at[rnd, pl.ds(0, len(peers))], sc_sem, rnd).wait_send()

        @pl.when(grid.owner)
        def _():
            all_in(pay.at[rnd, pl.ds(0, CHUNKS - 1)], rs_sem, rnd).wait_send()
            all_in(recv.at[rnd], ag_sem, rnd).wait_send()

        @pl.when(jnp.logical_not(grid.owner))
        def _():
            all_in(pay.at[rnd], rs_sem, rnd).wait_send()


def solution(mesh):
    sizes = (4, 8, 2, 4)
    ny, nz, nc, nx = sizes
    assert dict(mesh.shape) == {"dom": ny * nz * nc, "kv": nx}
    atoms = nz * A
    others = nx * ny * nc - 1

    def local(
        node_feats, positions, species, halo_rows, neighbours, nbr_count, recip_vectors,
        w_msg, w_rad1, w_rad2, w_upd, w_out, chi_table, hard_table,
    ):
        operands = (
            node_feats, positions, species.reshape(1, A), halo_rows, neighbours.T, nbr_count.reshape(1, A),
            recip_vectors, w_msg, w_rad1, w_rad2, w_upd, w_out.reshape(1, A), chi_table.reshape(1, 2),
            hard_table.reshape(1, 2),
        )
        out = pl.pallas_call(
            functools.partial(kernel, sizes),
            out_shape=jax.ShapeDtypeStruct((2, A), F32),
            in_specs=[pl.BlockSpec(memory_space=pltpu.HBM)] * len(operands),
            out_specs=pl.BlockSpec(memory_space=pltpu.VMEM),
            scratch_shapes=[pltpu.VMEM(v.shape, v.dtype) for v in operands]
            + [
                pltpu.VMEM((TROWS, A), BF16),
                pltpu.VMEM((TROWS, A), BF16),
                pltpu.VMEM((2, TROWS, A), BF16),
                pltpu.VMEM((nz, 8, A), F32),
                pltpu.VMEM((nz, 8, A), F32),
                pltpu.VMEM((TROWS, 2 * A), BF16),
                pltpu.VMEM((NBR, A), I32),
                pltpu.VMEM((4, A, A), F32),
                pltpu.VMEM((A, A), BF16),
                pltpu.VMEM((2 * A, A), BF16),
                pltpu.VMEM((A, 3 * A), BF16),
                pltpu.VMEM((2 * HALF, atoms), BF16),
                pltpu.VMEM((32, atoms), F32),
                pltpu.VMEM((1, atoms), F32),
                pltpu.VMEM((128, atoms), BF16),
                pltpu.VMEM((2, atoms), F32),
                pltpu.VMEM((2, atoms), F32),
                pltpu.VMEM((2, atoms), F32),
                pltpu.VMEM((ITERS, CHUNKS, 16, A), jnp.int16),
                pltpu.VMEM((ITERS, others, 16, A), jnp.int16),
                pltpu.VMEM((ITERS, CHUNKS, 16, A), jnp.int16),
                pltpu.VMEM((ITERS, others + 1, 1, A), F32),
                pltpu.VMEM((32, HALF), F32),
                pltpu.VMEM((3, 16, A), F32),
                pltpu.VMEM((3, 16, A), F32),
                pltpu.VMEM((6, 64, A), F32),
                pltpu.SemaphoreType.DMA((4,)),
                pltpu.SemaphoreType.DMA((2,)),
                pltpu.SemaphoreType.DMA((2,)),
                pltpu.SemaphoreType.DMA((2, ITERS)),
                pltpu.SemaphoreType.DMA((2, ITERS)),
                pltpu.SemaphoreType.DMA((2, ITERS)),
                pltpu.SemaphoreType.DMA((len(operands),)),
            ],
            compiler_params=pltpu.CompilerParams(
                collective_id=0, has_side_effects=True, vmem_limit_bytes=60 * 1024 * 1024
            ),
        )(*operands)
        return out[0], out[1]

    both = ("dom", "kv")
    return jax.shard_map(
        local,
        mesh=mesh,
        in_specs=(
            P(both, None), P(None, both), P(both), P(both, None), P(both, None), P(both),
            P(), P(), P(), P(), P(), P(), P(), P(),
        ),
        out_specs=(P(both), P(both)),
        check_vma=False,
    )
```

```python
import functools
import math

import jax
import jax.numpy as jnp
from jax import lax
from jax.experimental import pallas as pl
from jax.experimental.pallas import tpu as pltpu
from jax.sharding import PartitionSpec as P

MESH = pl.DeviceIdType.MESH
F32, BF16, I32 = jnp.float32, jnp.bfloat16, jnp.int32
ITERS = 4
SLAB_W = 9.0
SIDE = 20.0
A = 128
NBR = 32
HALF = 384
CHUNKS = 12
TROWS = 160
TURN = 2.0 * math.pi
SIN_C = [(-1.0) ** k * TURN ** (2 * k + 1) / math.factorial(2 * k + 1) for k in range(10)]
COS_C = [(-1.0) ** k * TURN ** (2 * k) / math.factorial(2 * k) for k in range(10)]


def dot(a, b):
    return jnp.dot(a, b, preferred_element_type=F32)


def dot_nt(a, b):
    return lax.dot_general(a, b, (((1,), (1,)), ((), ())), preferred_element_type=F32)


def sincos(turns):
    t = turns - jnp.round(turns)
    q = t * t
    s = jnp.full_like(q, SIN_C[-1])
    c = jnp.full_like(q, COS_C[-1])
    for k in range(len(SIN_C) - 2, -1, -1):
        s = s * q + SIN_C[k]
        c = c * q + COS_C[k]
    return s * t, c


def silu(v):
    h = 0.5 * v
    return h + h * jnp.tanh(h)


def transposed(v):
    return v.astype(F32).T


def coded(v):
    top = jnp.max(jnp.abs(v), axis=0, keepdims=True)
    power = jnp.ceil(jnp.log2(jnp.maximum(top, 1e-30) * 1.01)) - 15.0
    whole = jnp.round(v * jnp.exp2(-power))
    return jnp.where(iota(v.shape, 0) == 15, power, whole).astype(I32).astype(jnp.int16)


def decoded(q):
    v = q.astype(I32).astype(F32)
    return v * jnp.exp2(v[15:16])


def iota(shape, dim):
    return lax.broadcasted_iota(I32, shape, dim)


def ring(step, count):
    return min(step, count - step)


class Grid:
    def __init__(self, sizes):
        self.sizes = sizes
        ny, nz, nc, nx = sizes
        dom, x = lax.axis_index("dom"), lax.axis_index("kv")
        self.y, self.z, self.c, self.x = dom // (nz * nc), (dom // nc) % nz, dom % nc, x
        self.dom = dom
        steps = [(dx, dy, dc) for dx in range(nx) for dy in range(2) for dc in range(nc)]
        steps.sort(key=lambda s: (-(ring(s[0], nx) + s[1]), s))
        self.peers = []
        for dx, dy, dc in steps:
            if dx or dy or dc:
                px, py, pc = (x + dx) % nx, (self.y // 2) * 2 + (self.y + dy) % 2, (self.c + dc) % nc
                self.peers.append(({"dom": (py * nz + self.z) * nc + pc, "kv": px}, *self.share(px, py, pc)))
        self.chunk, self.owner = self.share(x, self.y, self.c)
        self.place = (self.y // 2) * nz + self.z
        steps = sorted([(dz, dy) for dz in range(nz) for dy in range(2)], key=lambda s: (-(ring(s[0], nz) + s[1]), s))
        self.column = []
        for dz, dy in steps:
            if dz or dy:
                py = self.y + dy * (ny - 1 - 2 * self.y)
                self.column.append({"dom": (py * nz + (self.z + dz) % nz) * nc + self.c, "kv": x})

    def share(self, x, y, c):
        ny, nz, nc, nx = self.sizes
        index = ((y % 2) * nx + x) * nc + c
        part = index % 4
        return (index // 4) * 3 + jnp.minimum(part, 2), part < 3

    def slab_peer(self, step):
        ny, nz, nc, nx = self.sizes
        count = ny * nz * nc * nx
        slab = (self.dom * nx + self.x + step + count) % count
        return {"dom": slab // nx, "kv": slab % nx}


def kernel(
    sizes,
    *refs,
):
    inputs, out_ref, arrived, scratch = refs[:14], refs[14], refs[15:29], refs[29:]
    (
        own_tab,
        packet,
        got,
        pos_all,
        en_all,
        nbr_tab,
        slots,
        acc,
        w_rad1_t,
        w_rad2_t,
        w_upd_t,
        table,
        xfac,
        hard_all,
        ff,
        res,
        direc,
        sol,
        pay,
        recv,
        full,
        scal,
        present,
        w_sum,
        w_dif,
        s_dir,
        halo_sem,
        pos_sem,
        en_sem,
        rs_sem,
        ag_sem,
        sc_sem,
        in_sem,
    ) = scratch
    (
        feats_ref, pos_ref, species_ref, halo_ref, nbr_ref, count_ref, recip_ref, w_msg_ref, w_rad1_ref, w_rad2_ref,
        w_upd_ref, w_out_ref, chi_ref, hard_ref,
    ) = arrived
    grid = Grid(sizes)
    gcount = 2 * sizes[1]
    gid = grid.place
    atoms = gcount * A
    peers, column = grid.peers, grid.column
    atoms_total = atoms * (len(peers) + 1)
    box_x = (atoms_total // A) * SLAB_W
    kvec = recip_ref.shape[1]

    loads = [pltpu.make_async_copy(src, dst, in_sem.at[i]) for i, (src, dst) in enumerate(zip(inputs, arrived))]
    for i in (0, 7, 1, 3, 2, 13, 4, 5, 6, 8, 9, 10, 11, 12):
        loads[i].start()

    barrier = pltpu.get_barrier_semaphore()
    partners = [grid.slab_peer(-1), grid.slab_peer(1)] + column + [device for device, _, _ in peers]
    for device in partners:
        pl.semaphore_signal(barrier, inc=1, device_id=device, device_id_type=MESH)

    def remote(src, dst, send, recv_, device):
        return pltpu.make_async_remote_copy(
            src_ref=src, dst_ref=dst, send_sem=send, recv_sem=recv_, device_id=device, device_id_type=MESH
        )

    for i in (0, 1, 2, 3, 7, 13):
        loads[i].wait()
    species = species_ref[...]
    hard = hard_ref[...]
    hardness = jnp.where(species == 0, hard[0:1, 0:1], hard[0:1, 1:2])
    pos = jnp.concatenate([pos_ref[...], jnp.zeros((5, A), F32)], axis=0)
    pos_all[gid] = jnp.concatenate([pos_ref[...], hardness, jnp.zeros((4, A), F32)], axis=0)
    proj_t = dot(feats_ref[...], w_msg_ref[...]).T
    hi = pos.astype(BF16).astype(F32)
    mid = (pos - hi).astype(BF16).astype(F32)
    low = pos - hi - mid
    own_tab[...] = jnp.concatenate([proj_t, hi, mid, low, jnp.zeros((8, A), F32)], axis=0).astype(BF16)
    halo = jnp.concatenate([halo_ref[...], halo_ref[...]], axis=1)
    pick = jnp.where(iota((A, A), 0) == halo, 1.0, 0.0).astype(BF16)
    packet[...] = dot(own_tab[...], pick).astype(BF16)

    pl.semaphore_wait(barrier, len(partners))

    to_left = remote(packet, got.at[1], halo_sem.at[0], halo_sem.at[3], grid.slab_peer(-1))
    to_right = remote(packet, got.at[0], halo_sem.at[1], halo_sem.at[2], grid.slab_peer(1))
    to_left.start()
    to_right.start()
    for device in column:
        remote(pos_all.at[gid], pos_all.at[gid], pos_sem.at[0], pos_sem.at[1], device).start()

    for i in (4, 5, 6, 8, 9, 10, 11, 12):
        loads[i].wait()
    w_rad1_t[...] = jnp.concatenate(
        [transposed(jnp.concatenate([w_rad1_ref[...].astype(F32), jnp.zeros((120, A), F32)], axis=0))], axis=1
    ).astype(BF16)
    for i in range(2):
        w_rad2_t[pl.ds(i * A, A), :] = transposed(w_rad2_ref[:, i * A : (i + 1) * A]).astype(BF16)
    for i in range(3):
        w_upd_t[:, pl.ds(i * A, A)] = transposed(w_upd_ref[i * A : (i + 1) * A, :]).astype(BF16)
    index = nbr_ref[...]
    place = jnp.where(index < A, index, jnp.where(index < A + 32, index + 32, index - 32))
    slots[...] = jnp.where(iota((NBR, A), 0) < count_ref[...], place, -1)
    nbr_tab[:, 0:A] = own_tab[...]
    feats_t = transposed(feats_ref[...])

    k_step = 2048 if kvec % 2048 == 0 else kvec
    present[...] = jnp.zeros((32, HALF), F32)

    def count_triples(step, carry):
        m = recip_ref[:, pl.ds(pl.multiple_of(step * k_step, 128), k_step)]
        mx, my, mz = m[0:1], m[1:2], m[2:3]
        flip = jnp.where((my < 0) | ((my == 0) & (mz < 0)), -1, 1)
        mx, my, mz = mx * flip, my * flip, mz * flip + 13
        row = jnp.where(mx >= 0, mx, 16 - mx)
        column = jnp.where(mz < 24, my * 24 + mz, 336 + (mz - 24) * 16 + my)
        hot_row = jnp.where(iota((32, k_step), 0) == row, 1.0, 0.0).astype(BF16)
        hot_col = jnp.where(iota((HALF, k_step), 0) == column, 1.0, 0.0).astype(BF16)
        present[...] += dot_nt(hot_row, hot_col)
        return carry

    k_steps = kvec // k_step
    H1, H2 = k_steps // 4, 3 * k_steps // 4
    lax.fori_loop(0, H1, count_triples, 0)

    to_left.wait_send()
    to_right.wait_send()
    to_left.wait_recv()
    to_right.wait_recv()
    from_right, from_left = got[1].astype(F32), got[0].astype(F32)
    nbr_tab[:, A : 2 * A] = jnp.where(iota((TROWS, A), 1) < 32, from_right, from_left).astype(BF16)

    group = 16
    wide = group * A
    acc[...] = jnp.zeros(acc.shape, F32)
    own_pos = jnp.concatenate([pos] * group, axis=1)
    axis_row = iota((8, 1), 0)
    length = jnp.where(axis_row == 0, box_x, SIDE)
    live_row = axis_row < 3

    def messages(step, carry):
        here = jnp.concatenate([slots[pl.ds(step * group + s, 1), :] for s in range(group)], axis=1)
        hot = jnp.where(iota((2 * A, wide), 0) == here, 1.0, 0.0).astype(BF16)
        found = dot(nbr_tab[...], hot)
        proj = found[0:A]
        offset = found[A : A + 8] + found[A + 8 : A + 16] + found[A + 16 : A + 24] - own_pos
        offset = jnp.where(
            offset > 0.5 * length, offset - length, jnp.where(offset < -0.5 * length, offset + length, offset)
        )
        offset = jnp.where(live_row, offset, 0.0)
        square = jnp.sum(offset * offset, axis=0, keepdims=True) + 0.25
        inverse = lax.rsqrt(square)
        unit = offset * inverse
        distance = square * inverse
        centre = 1.0 + 1.25 * iota((8, 1), 0).astype(F32)
        scaled = (distance - centre) / 1.25
        basis = jnp.exp(-(scaled * scaled))
        basis = jnp.concatenate([basis, jnp.zeros((A - 8, wide), F32)], axis=0).astype(BF16)
        hidden = silu(dot(w_rad1_t[...], basis)).astype(BF16)
        radial = dot(w_rad2_t[...], hidden)

        def fold(v):
            return functools.reduce(jnp.add, [v[:, s * A : (s + 1) * A] for s in range(group)])

        acc[0] += fold(radial[0:A] * proj)
        carried = radial[A : 2 * A] * proj
        for c in range(3):
            acc[c + 1] += fold(carried * unit[c : c + 1])
        return carry

    lax.fori_loop(0, NBR // group, messages, 0, unroll=True)
    scale = 1.0 / math.sqrt(NBR)
    vec = [acc[c + 1] * scale for c in range(3)]
    vec_square = vec[0] * vec[0] + vec[1] * vec[1] + vec[2] * vec[2]
    joined = jnp.concatenate([acc[0] * scale, vec_square, feats_t], axis=0).astype(BF16)
    update = silu(dot(w_upd_t[...], joined)).astype(BF16)
    w_out = jnp.broadcast_to(w_out_ref[...].astype(F32), (16, A)).astype(BF16)
    chi = chi_ref[...]
    electroneg = dot(w_out, update)[0:1] + jnp.where(species == 0, chi[0:1, 0:1], chi[0:1, 1:2])
    out_ref[0:1, :] = electroneg
    en_all[gid] = jnp.broadcast_to(electroneg, (8, A))
    for device in column:
        remote(en_all.at[gid], en_all.at[gid], en_sem.at[0], en_sem.at[1], device).start()

    def gathered(ref, sem):
        return remote(ref.at[pl.ds(0, gcount - 1)], ref.at[pl.ds(0, gcount - 1)], sem.at[0], sem.at[1], column[0])

    pos_done = gathered(pos_all, pos_sem)
    pos_done.wait_recv()

    def build(step, carry):
        lanes = pl.ds(pl.multiple_of(step * A, A), A)
        tile = pos_all[step]
        x, y, z = tile[0:1] / box_x, tile[1:2] / SIDE, tile[2:3] / SIDE
        hard_all[:, lanes] = tile[3:4]
        row16 = iota((16, A), 0)
        sx, cx = sincos(row16.astype(F32) * x)
        xfac[:, lanes] = jnp.where(jnp.concatenate([row16, row16], axis=0) < 14, jnp.concatenate([cx, sx], axis=0), 0.0)
        sy, cy = sincos(row16.astype(F32) * y)
        sz, cz = sincos((iota((32, A), 0) - 13).astype(F32) * z)
        cos_rows, sin_rows = [], []
        for i in range(14):
            a, b = cy[i : i + 1], sy[i : i + 1]
            cos_rows.append(a * cz[0:24] - b * sz[0:24])
            sin_rows.append(b * cz[0:24] + a * sz[0:24])
        for j in range(24, 27):
            a, b = cz[j : j + 1], sz[j : j + 1]
            cos_rows.append(a * cy - b * sy)
            sin_rows.append(b * cy + a * sy)
        table[0:HALF, lanes] = jnp.concatenate(cos_rows, axis=0).astype(BF16)
        table[HALF : 2 * HALF, lanes] = jnp.concatenate(sin_rows, axis=0).astype(BF16)
        return carry

    lax.fori_loop(0, gcount, build, 0)
    lax.fori_loop(H1, H2, count_triples, 0)

    en_done = gathered(en_all, en_sem)
    en_done.wait_recv()

    def start_residual(step, carry):
        lanes = pl.ds(pl.multiple_of(step * A, A), A)
        tile = en_all[step]
        res[:, lanes] = jnp.where(iota((2, A), 0) == 0, -tile[0:2], 1.0)
        return carry

    lax.fori_loop(0, gcount, start_residual, 0)
    sol[...] = jnp.zeros(sol.shape, F32)
    direc[...] = jnp.zeros(direc.shape, F32)
    s_dir[...] = jnp.zeros(s_dir.shape, F32)

    row64 = iota((64, A), 0)
    row16 = iota((16, A), 0)
    lane1 = iota((1, A), 1)

    def lane_sum(v):
        return jnp.sum(v, axis=1, keepdims=True)

    def all_in(ref, sem, rnd):
        return remote(ref, ref, sem.at[0, rnd], sem.at[1, rnd], column[0])

    norm_old = dir_hard = dir_total = sol_total = None
    for rnd in range(ITERS):
        r, p, h = res[...], direc[...], hard_all[...]
        sums = [lane_sum(r * r), lane_sum(h * r * r), lane_sum(h * r * p), lane_sum(r)]
        for k in range(2):
            full_f = xfac[...] * r[k : k + 1]
            top = full_f.astype(BF16)
            ff[pl.ds(k * 32, 32), :] = top
            ff[pl.ds(64 + k * 32, 32), :] = (full_f - top.astype(F32)).astype(BF16)
        extra = jnp.zeros((1, A), F32)
        for k in range(2):
            for j in range(4):
                extra = jnp.where(lane1 == 4 * k + j, sums[j][k : k + 1], extra)
        scal[rnd, 0] = extra
        for j in range(3):
            s = dot_nt(ff[...], table[pl.ds(j * 256, 256), :])
            s = s[0:64] + s[64:128]
            for t in range(8):
                pay[rnd, 4 * j + t // 2, t % 2] = coded(s[(t % 4) * 16 : (t % 4) * 16 + 16, (t // 4) * A : (t // 4 + 1) * A])

        for k, (device, share, owns) in enumerate(peers):

            @pl.when(owns)
            def _():
                remote(pay.at[rnd, share], recv.at[rnd, k], rs_sem.at[0, rnd], rs_sem.at[1, rnd], device).start()

        for k, (device, _, _) in enumerate(peers):
            remote(scal.at[rnd, 0], scal.at[rnd, k + 1], sc_sem.at[0, rnd], sc_sem.at[1, rnd], device).start()

        if rnd == 0:
            lax.fori_loop(H2, k_steps, count_triples, 0)
            column_id = iota((1, HALF), 1)
            late = column_id - 336
            grid_y = jnp.where(late < 0, (column_id * 2731) >> 16, late & 15)
            grid_z = jnp.where(late < 0, column_id - grid_y * 24 - 13, 11 + (late >> 4))
            grid_x = iota((16, 1), 0)
            m_square = (grid_y * grid_y + grid_z * grid_z + grid_x * grid_x).astype(F32)
            weight = 16.0 / atoms_total * jnp.exp(-m_square / 400.0) / (1.0 + m_square / 16.0)
            plus, minus = present[0:16] * weight, present[16:32] * weight
            for i in range(3):
                lanes = slice(i * 128, (i + 1) * 128)
                w_sum[i] = (plus + minus)[:, lanes]
                w_dif[i] = (plus - minus)[:, lanes]

        @pl.when(grid.owner)
        def _():
            all_in(recv.at[rnd], rs_sem, rnd).wait_recv()
            for t in range(2):
                total = decoded(pay[rnd, grid.chunk, t])
                for k in range(len(peers)):
                    total = total + decoded(recv[rnd, k, t])
                full[rnd, grid.chunk, t] = coded(jnp.where(row16 < 14, total, 0.0))
            for device, _, _ in peers:
                mine = full.at[rnd, grid.chunk]
                remote(mine, mine, ag_sem.at[0, rnd], ag_sem.at[1, rnd], device).start()
            all_in(full.at[rnd, pl.ds(0, CHUNKS - 1)], ag_sem, rnd).wait_recv()

        @pl.when(jnp.logical_not(grid.owner))
        def _():
            all_in(full.at[rnd], ag_sem, rnd).wait_recv()

        all_in(scal.at[rnd, pl.ds(0, len(peers))], sc_sem, rnd).wait_recv()
        added = jnp.sum(scal[rnd], axis=0)

        def scalars(j):
            return jnp.concatenate([added[:, j : j + 1], added[:, 4 + j : 5 + j]], axis=0)

        norm, res_hard, cross, res_total = [scalars(j) for j in range(4)]
        if rnd == 0:
            dir_hard, dir_total = res_hard, res_total
            beta = jnp.zeros_like(norm)
        else:
            beta = norm / norm_old
            dir_hard = res_hard + 2.0 * beta * cross + beta * beta * dir_hard
            dir_total = res_total + beta * dir_total
        beta_rows = jnp.where(row64 < 32, beta[0:1], beta[1:2])
        s_all = []
        for i in range(6):
            s = jnp.concatenate([decoded(full[rnd, 2 * i + t // 2, t % 2]) for t in range(4)], axis=0)
            if rnd > 0:
                s = s + beta_rows * s_dir[i]
            s_dir[i] = s
            s_all.append(s)
        q_cos, q_sin = [], []
        for i in range(3):
            both, diff = w_sum[i], w_dif[i]
            for k, out in ((0, q_cos), (1, q_sin)):
                mine, other = s_all[3 * k + i], s_all[3 * (1 - k) + i]
                sign = -1.0 if k == 0 else 1.0
                parts = []
                for rhs in (0, 32):
                    for t in (0, 1):
                        same = mine[rhs + 16 * t : rhs + 16 * t + 16]
                        swap = other[rhs + 16 * (1 - t) : rhs + 16 * (1 - t) + 16]
                        sign = -1.0 if t == k else 1.0
                        parts.append(both * same + sign * (diff * swap))
                out.append(jnp.concatenate(parts, axis=0))
        q_all = q_cos + q_sin
        energy = functools.reduce(jnp.add, [q * s for q, s in zip(q_all, s_all)])
        energy = lane_sum(energy)
        energy = jnp.concatenate(
            [jnp.sum(energy[0:32], axis=0, keepdims=True), jnp.sum(energy[32:64], axis=0, keepdims=True)], axis=0
        )
        alpha = norm / (dir_hard + energy)
        p = r + beta * p
        sol[...] += alpha * p
        step_total = alpha * dir_total
        sol_total = step_total if rnd == 0 else sol_total + step_total
        norm_old = norm
        if rnd + 1 < ITERS:
            direc[...] = p
            q_full = jnp.concatenate(q_all, axis=1)
            top = q_full.astype(BF16)
            qq = jnp.concatenate([top, (q_full - top.astype(F32)).astype(BF16)], axis=0)
            piece = 512 if atoms % 512 == 0 else atoms
            for j in range(atoms // piece):
                lanes = pl.ds(j * piece, piece)
                g = dot(qq, table[:, lanes])
                g = g[0:64] + g[64:128]
                xf = xfac[:, lanes]
                pot = jnp.concatenate(
                    [jnp.sum(g[k * 32 : k * 32 + 32] * xf, axis=0, keepdims=True) for k in range(2)], axis=0
                )
                applied = hard_all[:, lanes] * direc[:, lanes] + pot
                res[:, lanes] = res[:, lanes] - alpha * applied

    ratio = sol_total[0:1] / sol_total[1:2]
    mine = sol[:, pl.ds(pl.multiple_of(gid * A, A), A)]
    out_ref[1:2, :] = mine[0:1] - ratio * mine[1:2]

    pos_done.wait_send()
    en_done.wait_send()
    for rnd in range(ITERS):
        all_in(scal.at[rnd, pl.ds(0, len(peers))], sc_sem, rnd).wait_send()

        @pl.when(grid.owner)
        def _():
            all_in(pay.at[rnd, pl.ds(0, CHUNKS - 1)], rs_sem, rnd).wait_send()
            all_in(recv.at[rnd], ag_sem, rnd).wait_send()

        @pl.when(jnp.logical_not(grid.owner))
        def _():
            all_in(pay.at[rnd], rs_sem, rnd).wait_send()


def solution(mesh):
    sizes = (4, 8, 2, 4)
    ny, nz, nc, nx = sizes
    assert dict(mesh.shape) == {"dom": ny * nz * nc, "kv": nx}
    gcount = 2 * nz
    atoms = gcount * A
    others = nx * 2 * nc - 1

    def local(
        node_feats, positions, species, halo_rows, neighbours, nbr_count, recip_vectors,
        w_msg, w_rad1, w_rad2, w_upd, w_out, chi_table, hard_table,
    ):
        operands = (
            node_feats, positions, species.reshape(1, A), halo_rows, neighbours.T, nbr_count.reshape(1, A),
            recip_vectors, w_msg, w_rad1, w_rad2, w_upd, w_out.reshape(1, A), chi_table.reshape(1, 2),
            hard_table.reshape(1, 2),
        )
        out = pl.pallas_call(
            functools.partial(kernel, sizes),
            out_shape=jax.ShapeDtypeStruct((2, A), F32),
            in_specs=[pl.BlockSpec(memory_space=pltpu.HBM)] * len(operands),
            out_specs=pl.BlockSpec(memory_space=pltpu.VMEM),
            scratch_shapes=[pltpu.VMEM(v.shape, v.dtype) for v in operands]
            + [
                pltpu.VMEM((TROWS, A), BF16),
                pltpu.VMEM((TROWS, A), BF16),
                pltpu.VMEM((2, TROWS, A), BF16),
                pltpu.VMEM((gcount, 8, A), F32),
                pltpu.VMEM((gcount, 8, A), F32),
                pltpu.VMEM((TROWS, 2 * A), BF16),
                pltpu.VMEM((NBR, A), I32),
                pltpu.VMEM((4, A, A), F32),
                pltpu.VMEM((A, A), BF16),
                pltpu.VMEM((2 * A, A), BF16),
                pltpu.VMEM((A, 3 * A), BF16),
                pltpu.VMEM((2 * HALF, atoms), BF16),
                pltpu.VMEM((32, atoms), F32),
                pltpu.VMEM((1, atoms), F32),
                pltpu.VMEM((128, atoms), BF16),
                pltpu.VMEM((2, atoms), F32),
                pltpu.VMEM((2, atoms), F32),
                pltpu.VMEM((2, atoms), F32),
                pltpu.VMEM((ITERS, CHUNKS, 2, 16, A), jnp.int16),
                pltpu.VMEM((ITERS, others, 2, 16, A), jnp.int16),
                pltpu.VMEM((ITERS, CHUNKS, 2, 16, A), jnp.int16),
                pltpu.VMEM((ITERS, others + 1, 1, A), F32),
                pltpu.VMEM((32, HALF), F32),
                pltpu.VMEM((3, 16, A), F32),
                pltpu.VMEM((3, 16, A), F32),
                pltpu.VMEM((6, 64, A), F32),
                pltpu.SemaphoreType.DMA((4,)),
                pltpu.SemaphoreType.DMA((2,)),
                pltpu.SemaphoreType.DMA((2,)),
                pltpu.SemaphoreType.DMA((2, ITERS)),
                pltpu.SemaphoreType.DMA((2, ITERS)),
                pltpu.SemaphoreType.DMA((2, ITERS)),
                pltpu.SemaphoreType.DMA((len(operands),)),
            ],
            compiler_params=pltpu.CompilerParams(
                collective_id=0, has_side_effects=True, vmem_limit_bytes=60 * 1024 * 1024
            ),
        )(*operands)
        return out[0], out[1]

    both = ("dom", "kv")
    return jax.shard_map(
        local,
        mesh=mesh,
        in_specs=(
            P(both, None), P(None, both), P(both), P(both, None), P(both, None), P(both),
            P(), P(), P(), P(), P(), P(), P(), P(),
        ),
        out_specs=(P(both), P(both)),
        check_vma=False,
    )
```

```python
import functools
import math

import jax
import jax.numpy as jnp
from jax import lax
from jax.experimental import pallas as pl
from jax.experimental.pallas import tpu as pltpu
from jax.sharding import PartitionSpec as P

MESH = pl.DeviceIdType.MESH
F32, BF16, I32 = jnp.float32, jnp.bfloat16, jnp.int32
ITERS = 4
SLAB_W = 9.0
SIDE = 20.0
A = 128
NBR = 32
HALF = 384
CHUNKS = 12
TROWS = 160
TURN = 2.0 * math.pi
SIN_C = [(-1.0) ** k * TURN ** (2 * k + 1) / math.factorial(2 * k + 1) for k in range(10)]
COS_C = [(-1.0) ** k * TURN ** (2 * k) / math.factorial(2 * k) for k in range(10)]


def dot(a, b):
    return jnp.dot(a, b, preferred_element_type=F32)


def dot_nt(a, b):
    return lax.dot_general(a, b, (((1,), (1,)), ((), ())), preferred_element_type=F32)


def sincos(turns):
    t = turns - jnp.round(turns)
    q = t * t
    s = jnp.full_like(q, SIN_C[-1])
    c = jnp.full_like(q, COS_C[-1])
    for k in range(len(SIN_C) - 2, -1, -1):
        s = s * q + SIN_C[k]
        c = c * q + COS_C[k]
    return s * t, c


def silu(v):
    h = 0.5 * v
    return h + h * jnp.tanh(h)


def transposed(v):
    return v.astype(F32).T


def coded(v):
    top = jnp.max(jnp.abs(v), axis=0, keepdims=True)
    power = jnp.ceil(jnp.log2(jnp.maximum(top, 1e-30) * 1.01)) - 15.0
    whole = jnp.round(v * jnp.exp2(-power))
    return jnp.where(iota(v.shape, 0) == 15, power, whole).astype(I32).astype(jnp.int16)


def decoded(q):
    v = q.astype(I32).astype(F32)
    return v * jnp.exp2(v[15:16])


def iota(shape, dim):
    return lax.broadcasted_iota(I32, shape, dim)


def ring(step, count):
    return min(step, count - step)


class Grid:
    def __init__(self, sizes):
        self.sizes = sizes
        ny, nz, nc, nx = sizes
        dom, x = lax.axis_index("dom"), lax.axis_index("kv")
        self.y, self.z, self.c, self.x = dom // (nz * nc), (dom // nc) % nz, dom % nc, x
        self.dom = dom
        steps = [(dx, dy, dc) for dx in range(nx) for dy in range(2) for dc in range(nc)]
        steps.sort(key=lambda s: (-(ring(s[0], nx) + s[1]), s))
        self.peers = []
        for dx, dy, dc in steps:
            if dx or dy or dc:
                px, py, pc = (x + dx) % nx, (self.y // 2) * 2 + (self.y + dy) % 2, (self.c + dc) % nc
                self.peers.append(({"dom": (py * nz + self.z) * nc + pc, "kv": px}, *self.share(px, py, pc)))
        self.chunk, self.owner = self.share(x, self.y, self.c)
        self.place = (self.y // 2) * nz + self.z
        steps = sorted([(dz, dy) for dz in range(nz) for dy in range(2)], key=lambda s: (-(ring(s[0], nz) + s[1]), s))
        self.column = []
        for dz, dy in steps:
            if dz or dy:
                py = self.y + dy * (ny - 1 - 2 * self.y)
                self.column.append({"dom": (py * nz + (self.z + dz) % nz) * nc + self.c, "kv": x})

    def share(self, x, y, c):
        ny, nz, nc, nx = self.sizes
        index = ((y % 2) * nx + x) * nc + c
        part = index % 4
        return (index // 4) * 3 + jnp.minimum(part, 2), part < 3

    def slab_peer(self, step):
        ny, nz, nc, nx = self.sizes
        count = ny * nz * nc * nx
        slab = (self.dom * nx + self.x + step + count) % count
        return {"dom": slab // nx, "kv": slab % nx}


def kernel(
    sizes,
    *refs,
):
    inputs, out_ref, arrived, scratch = refs[:14], refs[14], refs[15:29], refs[29:]
    (
        own_tab,
        packet,
        got,
        pos_all,
        en_all,
        nbr_tab,
        slots,
        acc,
        w_rad1_t,
        w_rad2_t,
        w_upd_t,
        table,
        xfac,
        hard_all,
        ff,
        res,
        direc,
        sol,
        pay,
        recv,
        full,
        scal,
        present,
        weights,
        s_dir,
        ends,
        ends_sent,
        halo_sem,
        pos_sem,
        en_sem,
        rs_sem,
        ag_sem,
        sc_sem,
        in_sem,
    ) = scratch
    (
        feats_ref, pos_ref, species_ref, halo_ref, nbr_ref, count_ref, recip_ref, w_msg_ref, w_rad1_ref, w_rad2_ref,
        w_upd_ref, w_out_ref, chi_ref, hard_ref,
    ) = arrived
    grid = Grid(sizes)
    gcount = 2 * sizes[1]
    gid = grid.place
    atoms = gcount * A
    peers, column = grid.peers, grid.column
    atoms_total = atoms * (len(peers) + 1)
    box_x = (atoms_total // A) * SLAB_W
    kvec = recip_ref.shape[1]

    loads = [pltpu.make_async_copy(src, dst, in_sem.at[i]) for i, (src, dst) in enumerate(zip(inputs, arrived))]
    barrier = pltpu.get_barrier_semaphore()
    partners = [grid.slab_peer(-1), grid.slab_peer(1)] + column + [device for device, _, _ in peers]
    for k, device in enumerate(partners):
        if k == 2:
            for i in (0, 7, 1, 3, 2, 13, 4, 5, 6, 8, 9, 10, 11, 12):
                loads[i].start()
        pl.semaphore_signal(barrier, inc=1, device_id=device, device_id_type=MESH)

    def remote(src, dst, send, recv_, device):
        return pltpu.make_async_remote_copy(
            src_ref=src, dst_ref=dst, send_sem=send, recv_sem=recv_, device_id=device, device_id_type=MESH
        )

    for i in (0, 1, 2, 3, 7, 13):
        loads[i].wait()
    species = species_ref[...]
    hard = hard_ref[...]
    hardness = jnp.where(species == 0, hard[0:1, 0:1], hard[0:1, 1:2])
    pos = jnp.concatenate([pos_ref[...], jnp.zeros((5, A), F32)], axis=0)
    pos_all[gid] = jnp.concatenate([pos_ref[...], hardness, jnp.zeros((4, A), F32)], axis=0)
    proj_t = dot(feats_ref[...], w_msg_ref[...]).T
    hi = pos.astype(BF16).astype(F32)
    mid = (pos - hi).astype(BF16).astype(F32)
    low = pos - hi - mid
    own_tab[...] = jnp.concatenate([proj_t, hi, mid, low, jnp.zeros((8, A), F32)], axis=0).astype(BF16)
    halo = jnp.concatenate([halo_ref[...], halo_ref[...]], axis=1)
    pick = jnp.where(iota((A, A), 0) == halo, 1.0, 0.0).astype(BF16)
    packet[...] = dot(own_tab[...], pick).astype(BF16)

    pl.semaphore_wait(barrier, len(partners))

    to_left = remote(packet, got.at[1], halo_sem.at[0], halo_sem.at[3], grid.slab_peer(-1))
    to_right = remote(packet, got.at[0], halo_sem.at[1], halo_sem.at[2], grid.slab_peer(1))
    to_left.start()
    to_right.start()
    for device in column:
        remote(pos_all.at[gid], pos_all.at[gid], pos_sem.at[0], pos_sem.at[1], device).start()

    for i in (4, 5, 6, 8, 9, 10, 11, 12):
        loads[i].wait()
    w_rad1_t[...] = jnp.concatenate(
        [transposed(jnp.concatenate([w_rad1_ref[...].astype(F32), jnp.zeros((120, A), F32)], axis=0))], axis=1
    ).astype(BF16)
    for i in range(2):
        w_rad2_t[pl.ds(i * A, A), :] = transposed(w_rad2_ref[:, i * A : (i + 1) * A]).astype(BF16)
    for i in range(3):
        w_upd_t[:, pl.ds(i * A, A)] = transposed(w_upd_ref[i * A : (i + 1) * A, :]).astype(BF16)
    index = nbr_ref[...]
    place = jnp.where(index < A, index, jnp.where(index < A + 32, index + 32, index - 32))
    slots[...] = jnp.where(iota((NBR, A), 0) < count_ref[...], place, -1)
    nbr_tab[:, 0:A] = own_tab[...]
    feats_t = transposed(feats_ref[...])

    k_step = 2048 if kvec % 2048 == 0 else kvec
    present[...] = jnp.zeros((32, HALF), F32)

    def count_triples(step, carry):
        m = recip_ref[:, pl.ds(pl.multiple_of(step * k_step, 128), k_step)]
        mx, my, mz = m[0:1], m[1:2], m[2:3]
        flip = jnp.where((my < 0) | ((my == 0) & (mz < 0)), -1, 1)
        mx, my, mz = mx * flip, my * flip, mz * flip + 13
        row = jnp.where(mx >= 0, mx, 16 - mx)
        column = jnp.where(mz < 24, my * 24 + mz, 336 + (mz - 24) * 16 + my)
        hot_row = jnp.where(iota((32, k_step), 0) == row, 1.0, 0.0).astype(BF16)
        hot_col = jnp.where(iota((HALF, k_step), 0) == column, 1.0, 0.0).astype(BF16)
        present[...] += dot_nt(hot_row, hot_col)
        return carry

    k_steps = kvec // k_step
    H1, H2 = k_steps // 4, 3 * k_steps // 4
    lax.fori_loop(0, H1, count_triples, 0)

    to_left.wait_send()
    to_right.wait_send()
    to_left.wait_recv()
    to_right.wait_recv()
    from_right, from_left = got[1].astype(F32), got[0].astype(F32)
    nbr_tab[:, A : 2 * A] = jnp.where(iota((TROWS, A), 1) < 32, from_right, from_left).astype(BF16)

    group = 16
    wide = group * A
    acc[...] = jnp.zeros(acc.shape, F32)
    own_pos = jnp.concatenate([pos] * group, axis=1)
    axis_row = iota((8, 1), 0)
    length = jnp.where(axis_row == 0, box_x, SIDE)
    live_row = axis_row < 3

    def messages(step, carry):
        here = jnp.concatenate([slots[pl.ds(step * group + s, 1), :] for s in range(group)], axis=1)
        hot = jnp.where(iota((2 * A, wide), 0) == here, 1.0, 0.0).astype(BF16)
        found = dot(nbr_tab[...], hot)
        proj = found[0:A]
        offset = found[A : A + 8] + found[A + 8 : A + 16] + found[A + 16 : A + 24] - own_pos
        offset = jnp.where(
            offset > 0.5 * length, offset - length, jnp.where(offset < -0.5 * length, offset + length, offset)
        )
        offset = jnp.where(live_row, offset, 0.0)
        square = jnp.sum(offset * offset, axis=0, keepdims=True) + 0.25
        inverse = lax.rsqrt(square)
        unit = offset * inverse
        distance = square * inverse
        centre = 1.0 + 1.25 * iota((8, 1), 0).astype(F32)
        scaled = (distance - centre) / 1.25
        basis = jnp.exp(-(scaled * scaled))
        basis = jnp.concatenate([basis, jnp.zeros((A - 8, wide), F32)], axis=0).astype(BF16)
        hidden = silu(dot(w_rad1_t[...], basis)).astype(BF16)
        radial = dot(w_rad2_t[...], hidden)

        def fold(v):
            return functools.reduce(jnp.add, [v[:, s * A : (s + 1) * A] for s in range(group)])

        acc[0] += fold(radial[0:A] * proj)
        carried = radial[A : 2 * A] * proj
        for c in range(3):
            acc[c + 1] += fold(carried * unit[c : c + 1])
        return carry

    lax.fori_loop(0, NBR // group, messages, 0, unroll=True)
    scale = 1.0 / math.sqrt(NBR)
    vec = [acc[c + 1] * scale for c in range(3)]
    vec_square = vec[0] * vec[0] + vec[1] * vec[1] + vec[2] * vec[2]
    joined = jnp.concatenate([acc[0] * scale, vec_square, feats_t], axis=0).astype(BF16)
    update = silu(dot(w_upd_t[...], joined)).astype(BF16)
    w_out = jnp.broadcast_to(w_out_ref[...].astype(F32), (16, A)).astype(BF16)
    chi = chi_ref[...]
    electroneg = dot(w_out, update)[0:1] + jnp.where(species == 0, chi[0:1, 0:1], chi[0:1, 1:2])
    out_ref[0:1, :] = electroneg
    en_all[gid] = jnp.broadcast_to(electroneg, (8, A))
    for device in column:
        remote(en_all.at[gid], en_all.at[gid], en_sem.at[0], en_sem.at[1], device).start()

    def gathered(ref, sem):
        return remote(ref.at[pl.ds(0, gcount - 1)], ref.at[pl.ds(0, gcount - 1)], sem.at[0], sem.at[1], column[0])

    pos_done = gathered(pos_all, pos_sem)
    pos_done.wait_recv()

    def build(step, carry):
        lanes = pl.ds(pl.multiple_of(step * A, A), A)
        tile = pos_all[step]
        x, y, z = tile[0:1] / box_x, tile[1:2] / SIDE, tile[2:3] / SIDE
        hard_all[:, lanes] = tile[3:4]
        row16 = iota((16, A), 0)
        sx, cx = sincos(row16.astype(F32) * x)
        xfac[:, lanes] = jnp.where(jnp.concatenate([row16, row16], axis=0) < 14, jnp.concatenate([cx, sx], axis=0), 0.0)
        sy, cy = sincos(row16.astype(F32) * y)
        sz, cz = sincos((iota((32, A), 0) - 13).astype(F32) * z)
        cos_rows, sin_rows = [], []
        for i in range(14):
            a, b = cy[i : i + 1], sy[i : i + 1]
            cos_rows.append(a * cz[0:24] - b * sz[0:24])
            sin_rows.append(b * cz[0:24] + a * sz[0:24])
        for j in range(24, 27):
            a, b = cz[j : j + 1], sz[j : j + 1]
            cos_rows.append(a * cy - b * sy)
            sin_rows.append(b * cy + a * sy)
        cos_b = jnp.concatenate(cos_rows, axis=0).astype(BF16)
        sin_b = jnp.concatenate(sin_rows, axis=0).astype(BF16)
        for i in range(3):
            table[2 * i * A : (2 * i + 1) * A, lanes] = cos_b[i * A : (i + 1) * A]
            table[(2 * i + 1) * A : (2 * i + 2) * A, lanes] = sin_b[i * A : (i + 1) * A]
        return carry

    lax.fori_loop(0, gcount, build, 0)
    lax.fori_loop(H1, H2, count_triples, 0)

    en_done = gathered(en_all, en_sem)
    en_done.wait_recv()

    def start_residual(step, carry):
        lanes = pl.ds(pl.multiple_of(step * A, A), A)
        tile = en_all[step]
        res[:, lanes] = jnp.where(iota((2, A), 0) == 0, -tile[0:2], 1.0)
        return carry

    lax.fori_loop(0, gcount, start_residual, 0)
    sol[...] = jnp.zeros(sol.shape, F32)
    direc[...] = jnp.zeros(direc.shape, F32)
    s_dir[...] = jnp.zeros(s_dir.shape, F32)

    row16 = iota((16, A), 0)
    lane1 = iota((1, A), 1)

    def lane_sum(v):
        return jnp.sum(v, axis=1, keepdims=True)

    def all_in(ref, sem, rnd):
        return remote(ref, ref, sem.at[0, rnd], sem.at[1, rnd], column[0])

    def shared(rnd):
        return full.at[rnd] if rnd + 1 < ITERS else ends

    norm_old = energy = dir_hard = dir_total = sol_total = None
    for rnd in range(ITERS):
        r, p, h = res[...], direc[...], hard_all[...]
        sums = [lane_sum(r * r), lane_sum(h * r * r), lane_sum(h * r * p), lane_sum(r)]
        for k in range(2):
            full_f = xfac[...] * r[k : k + 1]
            top = full_f.astype(BF16)
            ff[pl.ds(k * 32, 32), :] = top
            ff[pl.ds(64 + k * 32, 32), :] = (full_f - top.astype(F32)).astype(BF16)
        extra = jnp.zeros((1, A), F32)
        for k in range(2):
            for j in range(4):
                extra = jnp.where(lane1 == 4 * k + j, sums[j][k : k + 1], extra)
        scal[rnd, 0] = extra
        for j in range(3):
            s = dot_nt(table[pl.ds(j * 256, 256), :], ff[...]).T
            s = s[0:64] + s[64:128]
            for k in range(2):
                cc, sc = s[k * 32 : k * 32 + 16, 0:A], s[k * 32 + 16 : k * 32 + 32, 0:A]
                cs, ss = s[k * 32 : k * 32 + 16, A : 2 * A], s[k * 32 + 16 : k * 32 + 32, A : 2 * A]
                pay[rnd, 2 * j + k, 0] = coded(cc - ss)
                pay[rnd, 2 * j + k, 1] = coded(sc + cs)
                pay[rnd, 6 + 2 * j + k, 0] = coded(cc + ss)
                pay[rnd, 6 + 2 * j + k, 1] = coded(sc - cs)

        for k, (device, share, owns) in enumerate(peers):

            @pl.when(owns)
            def _():
                remote(pay.at[rnd, share], recv.at[rnd, k], rs_sem.at[0, rnd], rs_sem.at[1, rnd], device).start()

        for k, (device, _, _) in enumerate(peers):
            remote(scal.at[rnd, 0], scal.at[rnd, k + 1], sc_sem.at[0, rnd], sc_sem.at[1, rnd], device).start()

        if rnd == 0:
            lax.fori_loop(H2, k_steps, count_triples, 0)
            column_id = iota((1, HALF), 1)
            late = column_id - 336
            grid_y = jnp.where(late < 0, (column_id * 2731) >> 16, late & 15)
            grid_z = jnp.where(late < 0, column_id - grid_y * 24 - 13, 11 + (late >> 4))
            grid_x = iota((16, 1), 0)
            m_square = (grid_y * grid_y + grid_z * grid_z + grid_x * grid_x).astype(F32)
            weight = 16.0 / atoms_total * jnp.exp(-m_square / 400.0) / (1.0 + m_square / 16.0)
            plus, minus = present[0:16] * weight, present[16:32] * weight
            for i in range(3):
                lanes = slice(i * 128, (i + 1) * 128)
                weights[i] = plus[:, lanes]
                weights[3 + i] = minus[:, lanes]

        @pl.when(grid.owner)
        def _():
            all_in(recv.at[rnd], rs_sem, rnd).wait_recv()
            parts = []
            for t in range(2):
                total = decoded(pay[rnd, grid.chunk, t])
                for k in range(len(peers)):
                    total = total + decoded(recv[rnd, k, t])
                total = jnp.where(row16 < 14, total, 0.0)
                if rnd + 1 < ITERS:
                    full[rnd, grid.chunk, t] = coded(total)
                parts.append(total)
            if rnd + 1 < ITERS:
                mine = full.at[rnd, grid.chunk]
            else:
                w = weights[grid.chunk // 2]
                before = s_dir[grid.chunk]
                square = w * (parts[0] * parts[0] + parts[1] * parts[1])
                cross = w * (parts[0] * before[0:16] + parts[1] * before[16:32])
                ends[grid.chunk] = jnp.concatenate(
                    [jnp.sum(square, axis=0, keepdims=True), jnp.sum(cross, axis=0, keepdims=True)], axis=0
                )
                mine = ends.at[grid.chunk]
            for device, _, _ in peers:
                remote(mine, mine, ag_sem.at[0, rnd], ag_sem.at[1, rnd], device).start()
            all_in(shared(rnd).at[pl.ds(0, CHUNKS - 1)], ag_sem, rnd).wait_recv()

        @pl.when(jnp.logical_not(grid.owner))
        def _():
            all_in(shared(rnd), ag_sem, rnd).wait_recv()

        all_in(scal.at[rnd, pl.ds(0, len(peers))], sc_sem, rnd).wait_recv()
        added = jnp.sum(scal[rnd], axis=0)

        def scalars(j):
            return jnp.concatenate([added[:, j : j + 1], added[:, 4 + j : 5 + j]], axis=0)

        norm, res_hard, cross, res_total = [scalars(j) for j in range(4)]
        if rnd == 0:
            dir_hard, dir_total = res_hard, res_total
            beta = jnp.zeros_like(norm)
        else:
            beta = norm / norm_old
            dir_hard = res_hard + 2.0 * beta * cross + beta * beta * dir_hard
            dir_total = res_total + beta * dir_total
        if rnd + 1 < ITERS:
            q_all, energy = [], []
            for o in range(CHUNKS):
                s = jnp.concatenate([decoded(full[rnd, o, t]) for t in range(2)], axis=0)
                if rnd > 0:
                    s = s + beta[o % 2 : o % 2 + 1] * s_dir[o]
                s_dir[o] = s
                w = weights[o // 2]
                q_all.append(jnp.concatenate([w, w], axis=0) * s)
                energy.append(q_all[-1] * s)
            energy = [jnp.sum(functools.reduce(jnp.add, energy[k::2]), axis=0, keepdims=True) for k in range(2)]
            energy = lane_sum(jnp.concatenate(energy, axis=0))
        else:
            sums = [functools.reduce(jnp.add, [ends[o] for o in range(k, CHUNKS, 2)]) for k in range(2)]
            square = lane_sum(jnp.concatenate([v[0:1] for v in sums], axis=0))
            cross = lane_sum(jnp.concatenate([v[1:2] for v in sums], axis=0))
            energy = square + 2.0 * beta * cross + beta * beta * energy
        alpha = norm / (dir_hard + energy)
        p = r + beta * p
        sol[...] += alpha * p
        step_total = alpha * dir_total
        sol_total = step_total if rnd == 0 else sol_total + step_total
        norm_old = norm
        if rnd + 1 < ITERS:
            direc[...] = p
            tiles = []
            for i in range(3):
                cos_rows, sin_rows = [], []
                for k in range(2):
                    plus, minus = q_all[2 * i + k], q_all[6 + 2 * i + k]
                    less = plus - minus
                    cos_rows.append(plus + minus)
                    sin_rows += [less[16:32], -less[0:16]]
                tiles += [jnp.concatenate(cos_rows, axis=0), jnp.concatenate(sin_rows, axis=0)]
            q_full = jnp.concatenate(tiles, axis=1)
            top = q_full.astype(BF16)
            qq = jnp.concatenate([top, (q_full - top.astype(F32)).astype(BF16)], axis=0)
            piece = 512 if atoms % 512 == 0 else atoms
            for j in range(atoms // piece):
                lanes = pl.ds(j * piece, piece)
                g = dot(qq, table[:, lanes])
                g = g[0:64] + g[64:128]
                xf = xfac[:, lanes]
                pot = jnp.concatenate(
                    [jnp.sum(g[k * 32 : k * 32 + 32] * xf, axis=0, keepdims=True) for k in range(2)], axis=0
                )
                applied = hard_all[:, lanes] * direc[:, lanes] + pot
                res[:, lanes] = res[:, lanes] - alpha * applied

    ratio = sol_total[0:1] / sol_total[1:2]
    mine = sol[:, pl.ds(pl.multiple_of(gid * A, A), A)]
    out_ref[1:2, :] = mine[0:1] - ratio * mine[1:2]

    pos_done.wait_send()
    en_done.wait_send()
    for rnd in range(ITERS):
        all_in(scal.at[rnd, pl.ds(0, len(peers))], sc_sem, rnd).wait_send()

        @pl.when(grid.owner)
        def _():
            all_in(pay.at[rnd, pl.ds(0, CHUNKS - 1)], rs_sem, rnd).wait_send()
            sent = recv.at[rnd] if rnd + 1 < ITERS else ends_sent
            all_in(sent, ag_sem, rnd).wait_send()

        @pl.when(jnp.logical_not(grid.owner))
        def _():
            all_in(pay.at[rnd], rs_sem, rnd).wait_send()


def solution(mesh):
    sizes = (4, 8, 2, 4)
    ny, nz, nc, nx = sizes
    assert dict(mesh.shape) == {"dom": ny * nz * nc, "kv": nx}
    gcount = 2 * nz
    atoms = gcount * A
    others = nx * 2 * nc - 1

    def local(
        node_feats, positions, species, halo_rows, neighbours, nbr_count, recip_vectors,
        w_msg, w_rad1, w_rad2, w_upd, w_out, chi_table, hard_table,
    ):
        operands = (
            node_feats, positions, species.reshape(1, A), halo_rows, neighbours.T, nbr_count.reshape(1, A),
            recip_vectors, w_msg, w_rad1, w_rad2, w_upd, w_out.reshape(1, A), chi_table.reshape(1, 2),
            hard_table.reshape(1, 2),
        )
        out = pl.pallas_call(
            functools.partial(kernel, sizes),
            out_shape=jax.ShapeDtypeStruct((2, A), F32),
            in_specs=[pl.BlockSpec(memory_space=pltpu.HBM)] * len(operands),
            out_specs=pl.BlockSpec(memory_space=pltpu.VMEM),
            scratch_shapes=[pltpu.VMEM(v.shape, v.dtype) for v in operands]
            + [
                pltpu.VMEM((TROWS, A), BF16),
                pltpu.VMEM((TROWS, A), BF16),
                pltpu.VMEM((2, TROWS, A), BF16),
                pltpu.VMEM((gcount, 8, A), F32),
                pltpu.VMEM((gcount, 8, A), F32),
                pltpu.VMEM((TROWS, 2 * A), BF16),
                pltpu.VMEM((NBR, A), I32),
                pltpu.VMEM((4, A, A), F32),
                pltpu.VMEM((A, A), BF16),
                pltpu.VMEM((2 * A, A), BF16),
                pltpu.VMEM((A, 3 * A), BF16),
                pltpu.VMEM((2 * HALF, atoms), BF16),
                pltpu.VMEM((32, atoms), F32),
                pltpu.VMEM((1, atoms), F32),
                pltpu.VMEM((128, atoms), BF16),
                pltpu.VMEM((2, atoms), F32),
                pltpu.VMEM((2, atoms), F32),
                pltpu.VMEM((2, atoms), F32),
                pltpu.VMEM((ITERS, CHUNKS, 2, 16, A), jnp.int16),
                pltpu.VMEM((ITERS, others, 2, 16, A), jnp.int16),
                pltpu.VMEM((ITERS, CHUNKS, 2, 16, A), jnp.int16),
                pltpu.VMEM((ITERS, others + 1, 1, A), F32),
                pltpu.VMEM((32, HALF), F32),
                pltpu.VMEM((6, 16, A), F32),
                pltpu.VMEM((CHUNKS, 32, A), F32),
                pltpu.VMEM((CHUNKS, 2, A), F32),
                pltpu.VMEM((others, 2, A), F32),
                pltpu.SemaphoreType.DMA((4,)),
                pltpu.SemaphoreType.DMA((2,)),
                pltpu.SemaphoreType.DMA((2,)),
                pltpu.SemaphoreType.DMA((2, ITERS)),
                pltpu.SemaphoreType.DMA((2, ITERS)),
                pltpu.SemaphoreType.DMA((2, ITERS)),
                pltpu.SemaphoreType.DMA((len(operands),)),
            ],
            compiler_params=pltpu.CompilerParams(
                collective_id=0, has_side_effects=True, vmem_limit_bytes=60 * 1024 * 1024
            ),
        )(*operands)
        return out[0], out[1]

    both = ("dom", "kv")
    return jax.shard_map(
        local,
        mesh=mesh,
        in_specs=(
            P(both, None), P(None, both), P(both), P(both, None), P(both, None), P(both),
            P(), P(), P(), P(), P(), P(), P(), P(),
        ),
        out_specs=(P(both), P(both)),
        check_vma=False,
    )
```

```python
import functools
import math

import jax
import jax.numpy as jnp
from jax import lax
from jax.experimental import pallas as pl
from jax.experimental.pallas import tpu as pltpu
from jax.sharding import PartitionSpec as P

MESH = pl.DeviceIdType.MESH
F32, BF16, I32 = jnp.float32, jnp.bfloat16, jnp.int32
ITERS = 4
SLAB_W = 9.0
SIDE = 20.0
A = 128
NBR = 32
HALF = 384
CHUNKS = 12
TROWS = 160
TURN = 2.0 * math.pi
SIN_C = [(-1.0) ** k * TURN ** (2 * k + 1) / math.factorial(2 * k + 1) for k in range(10)]
COS_C = [(-1.0) ** k * TURN ** (2 * k) / math.factorial(2 * k) for k in range(10)]


def dot(a, b):
    return jnp.dot(a, b, preferred_element_type=F32)


def dot_nt(a, b):
    return lax.dot_general(a, b, (((1,), (1,)), ((), ())), preferred_element_type=F32)


def sincos(turns):
    t = turns - jnp.round(turns)
    q = t * t
    s = jnp.full_like(q, SIN_C[-1])
    c = jnp.full_like(q, COS_C[-1])
    for k in range(len(SIN_C) - 2, -1, -1):
        s = s * q + SIN_C[k]
        c = c * q + COS_C[k]
    return s * t, c


def silu(v):
    h = 0.5 * v
    return h + h * jnp.tanh(h)


def transposed(v):
    return v.astype(F32).T


def coded(v):
    top = jnp.max(jnp.abs(v), axis=0, keepdims=True)
    power = jnp.ceil(jnp.log2(jnp.maximum(top, 1e-30) * 1.01)) - 15.0
    whole = jnp.round(v * jnp.exp2(-power))
    return jnp.where(iota(v.shape, 0) == 15, power, whole).astype(I32).astype(jnp.int16)


def decoded(q):
    v = q.astype(I32).astype(F32)
    return v * jnp.exp2(v[15:16])


def iota(shape, dim):
    return lax.broadcasted_iota(I32, shape, dim)


def ring(step, count):
    return min(step, count - step)


class Grid:
    def __init__(self, sizes):
        self.sizes = sizes
        ny, nz, nc, nx = sizes
        dom, x = lax.axis_index("dom"), lax.axis_index("kv")
        self.y, self.z, self.c, self.x = dom // (nz * nc), (dom // nc) % nz, dom % nc, x
        self.dom = dom
        steps = [(dx, dy, dc) for dx in range(nx) for dy in range(2) for dc in range(nc)]
        steps.sort(key=lambda s: (-(ring(s[0], nx) + s[1]), s))
        self.peers = []
        for dx, dy, dc in steps:
            if dx or dy or dc:
                px, py, pc = (x + dx) % nx, (self.y // 2) * 2 + (self.y + dy) % 2, (self.c + dc) % nc
                self.peers.append(({"dom": (py * nz + self.z) * nc + pc, "kv": px}, *self.share(px, py, pc)))
        self.chunk, self.owner = self.share(x, self.y, self.c)
        self.place = (self.y // 2) * nz + self.z
        steps = sorted([(dz, dy) for dz in range(nz) for dy in range(2)], key=lambda s: (-(ring(s[0], nz) + s[1]), s))
        self.column = []
        for dz, dy in steps:
            if dz or dy:
                py = self.y + dy * (ny - 1 - 2 * self.y)
                self.column.append({"dom": (py * nz + (self.z + dz) % nz) * nc + self.c, "kv": x})

    def share(self, x, y, c):
        ny, nz, nc, nx = self.sizes
        index = ((y % 2) * nx + x) * nc + c
        part = index % 4
        return (index // 4) * 3 + jnp.minimum(part, 2), part < 3

    def slab_peer(self, step):
        ny, nz, nc, nx = self.sizes
        count = ny * nz * nc * nx
        slab = (self.dom * nx + self.x + step + count) % count
        return {"dom": slab // nx, "kv": slab % nx}


def kernel(
    sizes,
    *refs,
):
    inputs, out_ref, arrived, scratch = refs[:14], refs[14], refs[15:29], refs[29:]
    (
        own_tab,
        packet,
        got,
        pos_all,
        en_all,
        nbr_tab,
        slots,
        acc,
        w_rad1_t,
        w_rad2_t,
        w_upd_t,
        table,
        xfac,
        hard_all,
        ff,
        res,
        direc,
        sol,
        pay,
        recv,
        full,
        scal,
        present,
        weights,
        s_dir,
        ends,
        ends_sent,
        halo_sem,
        pos_sem,
        en_sem,
        rs_sem,
        ag_sem,
        sc_sem,
        in_sem,
    ) = scratch
    (
        feats_ref, pos_ref, species_ref, halo_ref, nbr_ref, count_ref, recip_ref, w_msg_ref, w_rad1_ref, w_rad2_ref,
        w_upd_ref, w_out_ref, chi_ref, hard_ref,
    ) = arrived
    grid = Grid(sizes)
    gcount = 2 * sizes[1]
    gid = grid.place
    atoms = gcount * A
    peers, column = grid.peers, grid.column
    atoms_total = atoms * (len(peers) + 1)
    box_x = (atoms_total // A) * SLAB_W
    kvec = recip_ref.shape[1]

    loads = [pltpu.make_async_copy(src, dst, in_sem.at[i]) for i, (src, dst) in enumerate(zip(inputs, arrived))]
    barrier = pltpu.get_barrier_semaphore()
    partners = [grid.slab_peer(-1), grid.slab_peer(1)] + column + [device for device, _, _ in peers]
    for k, device in enumerate(partners):
        if k == 2:
            for i in (0, 7, 1, 3, 2, 13, 4, 5, 6, 8, 9, 10, 11, 12):
                loads[i].start()
        pl.semaphore_signal(barrier, inc=1, device_id=device, device_id_type=MESH)

    def remote(src, dst, send, recv_, device):
        return pltpu.make_async_remote_copy(
            src_ref=src, dst_ref=dst, send_sem=send, recv_sem=recv_, device_id=device, device_id_type=MESH
        )

    for i in (0, 1, 2, 3, 7, 13):
        loads[i].wait()
    species = species_ref[...]
    hard = hard_ref[...]
    hardness = jnp.where(species == 0, hard[0:1, 0:1], hard[0:1, 1:2])
    pos = jnp.concatenate([pos_ref[...], jnp.zeros((5, A), F32)], axis=0)
    pos_all[gid] = jnp.concatenate([pos_ref[...], hardness, jnp.zeros((4, A), F32)], axis=0)
    proj_t = dot(feats_ref[...], w_msg_ref[...]).T
    hi = pos.astype(BF16).astype(F32)
    mid = (pos - hi).astype(BF16).astype(F32)
    low = pos - hi - mid
    own_tab[...] = jnp.concatenate([proj_t, hi, mid, low, jnp.zeros((8, A), F32)], axis=0).astype(BF16)
    halo = jnp.concatenate([halo_ref[...], halo_ref[...]], axis=1)
    pick = jnp.where(iota((A, A), 0) == halo, 1.0, 0.0).astype(BF16)
    packet[...] = dot(own_tab[...], pick).astype(BF16)

    pl.semaphore_wait(barrier, len(partners))

    to_left = remote(packet, got.at[1], halo_sem.at[0], halo_sem.at[3], grid.slab_peer(-1))
    to_right = remote(packet, got.at[0], halo_sem.at[1], halo_sem.at[2], grid.slab_peer(1))
    to_left.start()
    to_right.start()
    for device in column:
        remote(pos_all.at[gid], pos_all.at[gid], pos_sem.at[0], pos_sem.at[1], device).start()

    for i in (4, 5, 6, 8, 9, 10, 11, 12):
        loads[i].wait()
    w_rad1_t[...] = jnp.concatenate(
        [transposed(jnp.concatenate([w_rad1_ref[...].astype(F32), jnp.zeros((120, A), F32)], axis=0))], axis=1
    ).astype(BF16)
    for i in range(2):
        w_rad2_t[pl.ds(i * A, A), :] = transposed(w_rad2_ref[:, i * A : (i + 1) * A]).astype(BF16)
    for i in range(3):
        w_upd_t[:, pl.ds(i * A, A)] = transposed(w_upd_ref[i * A : (i + 1) * A, :]).astype(BF16)
    index = nbr_ref[...]
    place = jnp.where(index < A, index, jnp.where(index < A + 32, index + 32, index - 32))
    slots[...] = jnp.where(iota((NBR, A), 0) < count_ref[...], place, -1)
    nbr_tab[:, 0:A] = own_tab[...]
    feats_t = transposed(feats_ref[...])

    k_step = 2048 if kvec % 2048 == 0 else kvec
    present[...] = jnp.zeros((32, HALF), F32)

    def count_triples(step, carry):
        m = recip_ref[:, pl.ds(pl.multiple_of(step * k_step, 128), k_step)]
        mx, my, mz = m[0:1], m[1:2], m[2:3]
        flip = jnp.where((my < 0) | ((my == 0) & (mz < 0)), -1, 1)
        mx, my, mz = mx * flip, my * flip, mz * flip + 13
        row = jnp.where(mx >= 0, mx, 16 - mx)
        column = jnp.where(mz < 24, my * 24 + mz, 336 + (mz - 24) * 16 + my)
        hot_row = jnp.where(iota((32, k_step), 0) == row, 1.0, 0.0).astype(BF16)
        hot_col = jnp.where(iota((HALF, k_step), 0) == column, 1.0, 0.0).astype(BF16)
        present[...] += dot_nt(hot_row, hot_col)
        return carry

    k_steps = kvec // k_step
    H1, H2 = k_steps // 4, 3 * k_steps // 4
    lax.fori_loop(0, H1, count_triples, 0)

    to_left.wait_send()
    to_right.wait_send()
    to_left.wait_recv()
    to_right.wait_recv()
    from_right, from_left = got[1].astype(F32), got[0].astype(F32)
    nbr_tab[:, A : 2 * A] = jnp.where(iota((TROWS, A), 1) < 32, from_right, from_left).astype(BF16)

    group = 32
    wide = group * A
    acc[...] = jnp.zeros(acc.shape, F32)
    own_pos = jnp.concatenate([pos] * group, axis=1)
    axis_row = iota((8, 1), 0)
    length = jnp.where(axis_row == 0, box_x, SIDE)
    live_row = axis_row < 3

    def messages(step, carry):
        here = jnp.concatenate([slots[pl.ds(step * group + s, 1), :] for s in range(group)], axis=1)
        hot = jnp.where(iota((2 * A, wide), 0) == here, 1.0, 0.0).astype(BF16)
        found = dot(nbr_tab[...], hot)
        proj = found[0:A]
        offset = found[A : A + 8] + found[A + 8 : A + 16] + found[A + 16 : A + 24] - own_pos
        offset = jnp.where(
            offset > 0.5 * length, offset - length, jnp.where(offset < -0.5 * length, offset + length, offset)
        )
        offset = jnp.where(live_row, offset, 0.0)
        square = jnp.sum(offset * offset, axis=0, keepdims=True) + 0.25
        inverse = lax.rsqrt(square)
        unit = offset * inverse
        distance = square * inverse
        centre = 1.0 + 1.25 * iota((8, 1), 0).astype(F32)
        scaled = (distance - centre) / 1.25
        basis = jnp.exp(-(scaled * scaled))
        basis = jnp.concatenate([basis, jnp.zeros((A - 8, wide), F32)], axis=0).astype(BF16)
        hidden = silu(dot(w_rad1_t[...], basis)).astype(BF16)
        radial = dot(w_rad2_t[...], hidden)

        def fold(v):
            return functools.reduce(jnp.add, [v[:, s * A : (s + 1) * A] for s in range(group)])

        acc[0] += fold(radial[0:A] * proj)
        carried = radial[A : 2 * A] * proj
        for c in range(3):
            acc[c + 1] += fold(carried * unit[c : c + 1])
        return carry

    lax.fori_loop(0, NBR // group, messages, 0, unroll=True)
    scale = 1.0 / math.sqrt(NBR)
    vec = [acc[c + 1] * scale for c in range(3)]
    vec_square = vec[0] * vec[0] + vec[1] * vec[1] + vec[2] * vec[2]
    joined = jnp.concatenate([acc[0] * scale, vec_square, feats_t], axis=0).astype(BF16)
    update = silu(dot(w_upd_t[...], joined)).astype(BF16)
    w_out = jnp.broadcast_to(w_out_ref[...].astype(F32), (16, A)).astype(BF16)
    chi = chi_ref[...]
    electroneg = dot(w_out, update)[0:1] + jnp.where(species == 0, chi[0:1, 0:1], chi[0:1, 1:2])
    out_ref[0:1, :] = electroneg
    en_all[gid] = jnp.broadcast_to(electroneg, (8, A))
    for device in column:
        remote(en_all.at[gid], en_all.at[gid], en_sem.at[0], en_sem.at[1], device).start()

    def gathered(ref, sem):
        return remote(ref.at[pl.ds(0, gcount - 1)], ref.at[pl.ds(0, gcount - 1)], sem.at[0], sem.at[1], column[0])

    pos_done = gathered(pos_all, pos_sem)
    pos_done.wait_recv()

    def build(step, carry):
        lanes = pl.ds(pl.multiple_of(step * A, A), A)
        tile = pos_all[step]
        x, y, z = tile[0:1] / box_x, tile[1:2] / SIDE, tile[2:3] / SIDE
        hard_all[:, lanes] = tile[3:4]
        row16 = iota((16, A), 0)
        sx, cx = sincos(row16.astype(F32) * x)
        xfac[:, lanes] = jnp.where(jnp.concatenate([row16, row16], axis=0) < 14, jnp.concatenate([cx, sx], axis=0), 0.0)
        sy, cy = sincos(row16.astype(F32) * y)
        sz, cz = sincos((iota((32, A), 0) - 13).astype(F32) * z)
        cos_rows, sin_rows = [], []
        for i in range(14):
            a, b = cy[i : i + 1], sy[i : i + 1]
            cos_rows.append(a * cz[0:24] - b * sz[0:24])
            sin_rows.append(b * cz[0:24] + a * sz[0:24])
        for j in range(24, 27):
            a, b = cz[j : j + 1], sz[j : j + 1]
            cos_rows.append(a * cy - b * sy)
            sin_rows.append(b * cy + a * sy)
        cos_b = jnp.concatenate(cos_rows, axis=0).astype(BF16)
        sin_b = jnp.concatenate(sin_rows, axis=0).astype(BF16)
        for i in range(3):
            table[2 * i * A : (2 * i + 1) * A, lanes] = cos_b[i * A : (i + 1) * A]
            table[(2 * i + 1) * A : (2 * i + 2) * A, lanes] = sin_b[i * A : (i + 1) * A]
        return carry

    lax.fori_loop(0, gcount, build, 0)
    lax.fori_loop(H1, H2, count_triples, 0)

    en_done = gathered(en_all, en_sem)
    en_done.wait_recv()

    def start_residual(step, carry):
        lanes = pl.ds(pl.multiple_of(step * A, A), A)
        tile = en_all[step]
        res[:, lanes] = jnp.where(iota((2, A), 0) == 0, -tile[0:2], 1.0)
        return carry

    lax.fori_loop(0, gcount, start_residual, 0)
    sol[...] = jnp.zeros(sol.shape, F32)
    direc[...] = jnp.zeros(direc.shape, F32)
    s_dir[...] = jnp.zeros(s_dir.shape, F32)

    row16 = iota((16, A), 0)
    lane1 = iota((1, A), 1)

    def lane_sum(v):
        return jnp.sum(v, axis=1, keepdims=True)

    def all_in(ref, sem, rnd):
        return remote(ref, ref, sem.at[0, rnd], sem.at[1, rnd], column[0])

    def shared(rnd):
        return full.at[rnd] if rnd + 1 < ITERS else ends

    norm_old = energy = dir_hard = dir_total = sol_total = None
    for rnd in range(ITERS):
        r, p, h = res[...], direc[...], hard_all[...]
        sums = [lane_sum(r * r), lane_sum(h * r * r), lane_sum(h * r * p), lane_sum(r)]
        for k in range(2):
            full_f = xfac[...] * r[k : k + 1]
            top = full_f.astype(BF16)
            ff[pl.ds(k * 32, 32), :] = top
            ff[pl.ds(64 + k * 32, 32), :] = (full_f - top.astype(F32)).astype(BF16)
        extra = jnp.zeros((1, A), F32)
        for k in range(2):
            for j in range(4):
                extra = jnp.where(lane1 == 4 * k + j, sums[j][k : k + 1], extra)
        scal[rnd, 0] = extra
        for j in range(3):
            tiles = [dot_nt(table[pl.ds(j * 256 + t * A, A), :], ff[...]).T for t in range(2)]
            s = jnp.concatenate([tile[0:64] + tile[64:128] for tile in tiles], axis=1)
            for k in range(2):
                cc, sc = s[k * 32 : k * 32 + 16, 0:A], s[k * 32 + 16 : k * 32 + 32, 0:A]
                cs, ss = s[k * 32 : k * 32 + 16, A : 2 * A], s[k * 32 + 16 : k * 32 + 32, A : 2 * A]
                pay[rnd, 2 * j + k, 0] = coded(cc - ss)
                pay[rnd, 2 * j + k, 1] = coded(sc + cs)
                pay[rnd, 6 + 2 * j + k, 0] = coded(cc + ss)
                pay[rnd, 6 + 2 * j + k, 1] = coded(sc - cs)

        for k, (device, share, owns) in enumerate(peers):

            @pl.when(owns)
            def _():
                remote(pay.at[rnd, share], recv.at[rnd, k], rs_sem.at[0, rnd], rs_sem.at[1, rnd], device).start()

        for k, (device, _, _) in enumerate(peers):
            remote(scal.at[rnd, 0], scal.at[rnd, k + 1], sc_sem.at[0, rnd], sc_sem.at[1, rnd], device).start()

        if rnd == 0:
            lax.fori_loop(H2, k_steps, count_triples, 0)
            column_id = iota((1, HALF), 1)
            late = column_id - 336
            grid_y = jnp.where(late < 0, (column_id * 2731) >> 16, late & 15)
            grid_z = jnp.where(late < 0, column_id - grid_y * 24 - 13, 11 + (late >> 4))
            grid_x = iota((16, 1), 0)
            m_square = (grid_y * grid_y + grid_z * grid_z + grid_x * grid_x).astype(F32)
            weight = 16.0 / atoms_total * jnp.exp(-m_square / 400.0) / (1.0 + m_square / 16.0)
            plus, minus = present[0:16] * weight, present[16:32] * weight
            for i in range(3):
                lanes = slice(i * 128, (i + 1) * 128)
                weights[i] = plus[:, lanes]
                weights[3 + i] = minus[:, lanes]

        @pl.when(grid.owner)
        def _():
            all_in(recv.at[rnd], rs_sem, rnd).wait_recv()
            parts = []
            for t in range(2):
                total = decoded(pay[rnd, grid.chunk, t])
                for k in range(len(peers)):
                    total = total + decoded(recv[rnd, k, t])
                total = jnp.where(row16 < 14, total, 0.0)
                if rnd + 1 < ITERS:
                    full[rnd, grid.chunk, t] = coded(total)
                parts.append(total)
            if rnd + 1 < ITERS:
                mine = full.at[rnd, grid.chunk]
            else:
                w = weights[grid.chunk // 2]
                before = s_dir[grid.chunk]
                square = w * (parts[0] * parts[0] + parts[1] * parts[1])
                cross = w * (parts[0] * before[0:16] + parts[1] * before[16:32])
                ends[grid.chunk] = jnp.concatenate(
                    [jnp.sum(square, axis=0, keepdims=True), jnp.sum(cross, axis=0, keepdims=True)], axis=0
                )
                mine = ends.at[grid.chunk]
            for device, _, _ in peers:
                remote(mine, mine, ag_sem.at[0, rnd], ag_sem.at[1, rnd], device).start()
            all_in(shared(rnd).at[pl.ds(0, CHUNKS - 1)], ag_sem, rnd).wait_recv()

        @pl.when(jnp.logical_not(grid.owner))
        def _():
            all_in(shared(rnd), ag_sem, rnd).wait_recv()

        all_in(scal.at[rnd, pl.ds(0, len(peers))], sc_sem, rnd).wait_recv()
        added = jnp.sum(scal[rnd], axis=0)

        def scalars(j):
            return jnp.concatenate([added[:, j : j + 1], added[:, 4 + j : 5 + j]], axis=0)

        norm, res_hard, cross, res_total = [scalars(j) for j in range(4)]
        if rnd == 0:
            dir_hard, dir_total = res_hard, res_total
            beta = jnp.zeros_like(norm)
        else:
            beta = norm / norm_old
            dir_hard = res_hard + 2.0 * beta * cross + beta * beta * dir_hard
            dir_total = res_total + beta * dir_total
        if rnd + 1 < ITERS:
            q_all, energy = [], []
            for o in range(CHUNKS):
                s = jnp.concatenate([decoded(full[rnd, o, t]) for t in range(2)], axis=0)
                if rnd > 0:
                    s = s + beta[o % 2 : o % 2 + 1] * s_dir[o]
                s_dir[o] = s
                w = weights[o // 2]
                q_all.append(jnp.concatenate([w, w], axis=0) * s)
                energy.append(q_all[-1] * s)
            energy = [jnp.sum(functools.reduce(jnp.add, energy[k::2]), axis=0, keepdims=True) for k in range(2)]
            energy = lane_sum(jnp.concatenate(energy, axis=0))
        else:
            sums = [functools.reduce(jnp.add, [ends[o] for o in range(k, CHUNKS, 2)]) for k in range(2)]
            square = lane_sum(jnp.concatenate([v[0:1] for v in sums], axis=0))
            cross = lane_sum(jnp.concatenate([v[1:2] for v in sums], axis=0))
            energy = square + 2.0 * beta * cross + beta * beta * energy
        alpha = norm / (dir_hard + energy)
        p = r + beta * p
        sol[...] += alpha * p
        step_total = alpha * dir_total
        sol_total = step_total if rnd == 0 else sol_total + step_total
        norm_old = norm
        if rnd + 1 < ITERS:
            direc[...] = p
            tiles = []
            for i in range(3):
                cos_rows, sin_rows = [], []
                for k in range(2):
                    plus, minus = q_all[2 * i + k], q_all[6 + 2 * i + k]
                    less = plus - minus
                    cos_rows.append(plus + minus)
                    sin_rows += [less[16:32], -less[0:16]]
                tiles += [jnp.concatenate(cos_rows, axis=0), jnp.concatenate(sin_rows, axis=0)]
            q_full = jnp.concatenate(tiles, axis=1)
            top = q_full.astype(BF16)
            qq = jnp.concatenate([top, (q_full - top.astype(F32)).astype(BF16)], axis=0)
            piece = 512 if atoms % 512 == 0 else atoms
            for j in range(atoms // piece):
                lanes = pl.ds(j * piece, piece)
                g = dot(qq, table[:, lanes])
                g = g[0:64] + g[64:128]
                xf = xfac[:, lanes]
                pot = jnp.concatenate(
                    [jnp.sum(g[k * 32 : k * 32 + 32] * xf, axis=0, keepdims=True) for k in range(2)], axis=0
                )
                applied = hard_all[:, lanes] * direc[:, lanes] + pot
                res[:, lanes] = res[:, lanes] - alpha * applied

    ratio = sol_total[0:1] / sol_total[1:2]
    mine = sol[:, pl.ds(pl.multiple_of(gid * A, A), A)]
    out_ref[1:2, :] = mine[0:1] - ratio * mine[1:2]

    pos_done.wait_send()
    en_done.wait_send()
    for rnd in range(ITERS):
        all_in(scal.at[rnd, pl.ds(0, len(peers))], sc_sem, rnd).wait_send()

        @pl.when(grid.owner)
        def _():
            all_in(pay.at[rnd, pl.ds(0, CHUNKS - 1)], rs_sem, rnd).wait_send()
            sent = recv.at[rnd] if rnd + 1 < ITERS else ends_sent
            all_in(sent, ag_sem, rnd).wait_send()

        @pl.when(jnp.logical_not(grid.owner))
        def _():
            all_in(pay.at[rnd], rs_sem, rnd).wait_send()


def solution(mesh):
    sizes = (4, 8, 2, 4)
    ny, nz, nc, nx = sizes
    assert dict(mesh.shape) == {"dom": ny * nz * nc, "kv": nx}
    gcount = 2 * nz
    atoms = gcount * A
    others = nx * 2 * nc - 1

    def local(
        node_feats, positions, species, halo_rows, neighbours, nbr_count, recip_vectors,
        w_msg, w_rad1, w_rad2, w_upd, w_out, chi_table, hard_table,
    ):
        operands = (
            node_feats, positions, species.reshape(1, A), halo_rows, neighbours.T, nbr_count.reshape(1, A),
            recip_vectors, w_msg, w_rad1, w_rad2, w_upd, w_out.reshape(1, A), chi_table.reshape(1, 2),
            hard_table.reshape(1, 2),
        )
        out = pl.pallas_call(
            functools.partial(kernel, sizes),
            out_shape=jax.ShapeDtypeStruct((2, A), F32),
            in_specs=[pl.BlockSpec(memory_space=pltpu.HBM)] * len(operands),
            out_specs=pl.BlockSpec(memory_space=pltpu.VMEM),
            scratch_shapes=[pltpu.VMEM(v.shape, v.dtype) for v in operands]
            + [
                pltpu.VMEM((TROWS, A), BF16),
                pltpu.VMEM((TROWS, A), BF16),
                pltpu.VMEM((2, TROWS, A), BF16),
                pltpu.VMEM((gcount, 8, A), F32),
                pltpu.VMEM((gcount, 8, A), F32),
                pltpu.VMEM((TROWS, 2 * A), BF16),
                pltpu.VMEM((NBR, A), I32),
                pltpu.VMEM((4, A, A), F32),
                pltpu.VMEM((A, A), BF16),
                pltpu.VMEM((2 * A, A), BF16),
                pltpu.VMEM((A, 3 * A), BF16),
                pltpu.VMEM((2 * HALF, atoms), BF16),
                pltpu.VMEM((32, atoms), F32),
                pltpu.VMEM((1, atoms), F32),
                pltpu.VMEM((128, atoms), BF16),
                pltpu.VMEM((2, atoms), F32),
                pltpu.VMEM((2, atoms), F32),
                pltpu.VMEM((2, atoms), F32),
                pltpu.VMEM((ITERS, CHUNKS, 2, 16, A), jnp.int16),
                pltpu.VMEM((ITERS, others, 2, 16, A), jnp.int16),
                pltpu.VMEM((ITERS, CHUNKS, 2, 16, A), jnp.int16),
                pltpu.VMEM((ITERS, others + 1, 1, A), F32),
                pltpu.VMEM((32, HALF), F32),
                pltpu.VMEM((6, 16, A), F32),
                pltpu.VMEM((CHUNKS, 32, A), F32),
                pltpu.VMEM((CHUNKS, 2, A), F32),
                pltpu.VMEM((others, 2, A), F32),
                pltpu.SemaphoreType.DMA((4,)),
                pltpu.SemaphoreType.DMA((2,)),
                pltpu.SemaphoreType.DMA((2,)),
                pltpu.SemaphoreType.DMA((2, ITERS)),
                pltpu.SemaphoreType.DMA((2, ITERS)),
                pltpu.SemaphoreType.DMA((2, ITERS)),
                pltpu.SemaphoreType.DMA((len(operands),)),
            ],
            compiler_params=pltpu.CompilerParams(
                collective_id=0, has_side_effects=True, vmem_limit_bytes=60 * 1024 * 1024
            ),
        )(*operands)
        return out[0], out[1]

    both = ("dom", "kv")
    return jax.shard_map(
        local,
        mesh=mesh,
        in_specs=(
            P(both, None), P(None, both), P(both), P(both, None), P(both, None), P(both),
            P(), P(), P(), P(), P(), P(), P(), P(),
        ),
        out_specs=(P(both), P(both)),
        check_vma=False,
    )
```
